32 devices in a mesh: obs: 4 (over y, x), par: 8 (over z, core).
Axes of the slice: x: 2, y: 2, z: 4, core: 2. Of those that a mesh axis runs over, the one named last changes fastest.
Arguments:
- design: bfloat16 [1024, 12288], P('obs', 'par'), may hold values from -3 to 3
- filter_taps: float32 [2, 512], replicated, may hold values from -0.4 to 5
- band_limit: int32 [2], replicated, may hold values from 128 to 512, as said below
- col_order: int32 [8], replicated, may hold values from 0 to 7, each once
Outputs:
- normal: float32 [12288, 12288], P('par', 'obs')
The draws below stay inside these ranges and needn't reach their ends.
Inputs may be any that keep to these rules, and one draw needn't show every extreme that they name: col_order names every parameter block once. `band_limit`: the first arc batch uses all 512 lags.
All inputs are finite; a program needn't handle non-finite values.
Results may differ from the reference program's by a relative error of at most 0.0051.
Values may be sent and summed in bfloat16 or wider, within the bound.
A program may use at most 128 MiB of HBM per device.

```python
import jax
import jax.numpy as jnp
from jax import lax

PAR_DEV = 1536
ARC_LEN = 512
ARCS = 2
OBS = 1024
PAR = 12288
N_PAR = 8


def draw_band_limit(key, part):
    rest = jax.random.randint(jax.random.fold_in(key, 17), (ARCS,), ARC_LEN // 4, ARC_LEN // 2 + 1)
    first = lax.broadcasted_iota(jnp.int32, (ARCS,), 0) == 0
    return jnp.where(first, jnp.full((ARCS,), ARC_LEN, jnp.int32), rest).astype(jnp.int32)


def draw_filter_taps(key, part):
    spread = 1.1 * (2.0 * ARC_LEN) ** (-0.5)
    rough_key = jax.random.fold_in(key, 31)
    lead_key = jax.random.fold_in(key, 37)
    rough = jax.random.normal(rough_key, (ARCS, ARC_LEN), jnp.float32) * spread
    lead = jax.random.uniform(lead_key, (ARCS, 1), jnp.float32, 3.5, 4.5)
    rough = jnp.clip(rough, -0.4, 0.4)
    first_lag = lax.broadcasted_iota(jnp.int32, (ARCS, ARC_LEN), 1) == 0
    return jnp.where(first_lag, jnp.broadcast_to(lead, (ARCS, ARC_LEN)), rough).astype(jnp.float32)


def steps_of(stream_key, dims, cuts, low, largest):
    level, own = 1.0, jax.random.fold_in(stream_key, 6)
    for position, shards_of in cuts:
        draws = jnp.exp(jax.random.uniform(jax.random.fold_in(own, position), (shards_of,), jnp.float32, low / len(cuts), largest / len(cuts)))
        level = level * jnp.repeat(draws, dims[position] // shards_of).reshape([-1 if axis == position else 1 for axis in range(len(dims))])
    return level


def normal_values(rng, dims, width, bound, pieces=(), kind=jnp.bfloat16):
    level = steps_of(rng, dims, pieces, -0.22, 0.18) if pieces else 1.0
    result = jax.random.normal(rng, dims, jnp.float32) * width * level
    return jnp.minimum(jnp.maximum(result, -bound), bound).astype(kind)


def setup_inputs(seed: int = 0) -> dict:
    arg_keys = jax.random.split(jax.random.key(seed), 5)
    return {
        "design": normal_values(arg_keys[0], (OBS, PAR), 0.5, 3.0, ((0, 4), (1, 8))),
        "filter_taps": draw_filter_taps(jax.random.fold_in(arg_keys[4], 71), 0),
        "band_limit": draw_band_limit(jax.random.fold_in(arg_keys[4], 71), 0),
        "col_order": jax.random.permutation(arg_keys[3], N_PAR).astype(jnp.int32),
    }


def arc_filters(filter_taps, band_limit):
    offsets = lax.broadcasted_iota(jnp.int32, (ARC_LEN, ARC_LEN), 0) - lax.broadcasted_iota(jnp.int32, (ARC_LEN, ARC_LEN), 1)
    distance = jnp.abs(offsets)

    def single(taps_row, limit_value):
        values = taps_row.astype(jnp.bfloat16)[distance]
        inside = distance < limit_value
        return jnp.where(inside, values, jnp.zeros_like(values))

    return jax.vmap(single)(filter_taps, band_limit)


def reference(design, filter_taps, band_limit, col_order):
    filters = arc_filters(filter_taps, band_limit)
    blocks = design.reshape(ARC_LEN, ARCS, PAR)
    filtered = jnp.einsum("ats,sap->tap", filters.astype(jnp.float32), blocks.astype(jnp.float32), precision=lax.Precision.HIGHEST)
    filtered = filtered.astype(jnp.bfloat16).reshape(OBS, PAR)
    widened = filtered.astype(jnp.float32)
    reordered = widened.reshape(OBS, N_PAR, PAR_DEV)[:, col_order, :].reshape(OBS, PAR)
    return jnp.dot(widened.T, reordered, precision=lax.Precision.HIGHEST) / OBS
```

```python
import functools

import jax
import jax.numpy as jnp
from jax import lax
from jax.experimental import pallas as pl
from jax.experimental.pallas import tpu as pltpu
from jax.sharding import PartitionSpec as P

MESH = pl.DeviceIdType.MESH
LANES = 128


def build_filters(taps_ref, limit_ref, filt_ref):
    arcs, arc_len = taps_ref.shape
    tiles = arc_len // LANES
    row = lax.broadcasted_iota(jnp.int32, (LANES, 2 * LANES), 0)
    upper = lax.broadcasted_iota(jnp.int32, (LANES, LANES), 1) >= lax.broadcasted_iota(
        jnp.int32, (LANES, LANES), 0
    )
    lag = lax.broadcasted_iota(jnp.int32, (1, arc_len), 1)
    for a in range(arcs):
        taps = taps_ref[a : a + 1, :].astype(jnp.bfloat16).astype(jnp.float32)
        taps = jnp.where(lag < limit_ref[a], taps, 0.0)
        for d in range(tiles):
            before = taps[:, (d - 1) * LANES : d * LANES] if d else jnp.zeros((1, LANES), jnp.float32)
            strip = jnp.concatenate([before, taps[:, d * LANES : (d + 1) * LANES]], axis=1)
            strip = jnp.broadcast_to(strip, (LANES, 2 * LANES))
            step = 1
            while step < LANES:
                strip = jnp.where((row & step) != 0, pltpu.roll(strip, step, 1), strip)
                step *= 2
            tile = strip[:, LANES:]
            mirrored = tile.T
            if d == 0:
                tile = jnp.where(upper, tile, mirrored)
            tile_low, mirrored_low = tile.astype(jnp.bfloat16), mirrored.astype(jnp.bfloat16)
            for i in range(tiles - d):
                lo, hi = pl.ds(i * LANES, LANES), pl.ds((i + d) * LANES, LANES)
                filt_ref[a, lo, hi] = tile_low
                if d:
                    filt_ref[a, hi, lo] = mirrored_low


def gather_kernel(
    obs_size, par_size, width,
    design_ref, taps_ref, limit_ref, order_ref,
    own_ref, part_ref,
    raw_ref, filt_ref, stage_ref, mixed_ref,
    place_sem, across_s, across_r, line_s, line_r,
    own_s, own_r, swap_s, swap_r, back_s, back_r,
    *pools,
):
    arcs, arc_len, columns = raw_ref.shape
    rows = design_ref.shape[0]
    epochs = rows // arcs
    half = columns // 2
    chunks = half // width
    blocks_per = par_size // obs_size
    chips = par_size // 2
    hops = chips - 1
    o, p = lax.axis_index("obs"), lax.axis_index("par")
    k, core = p // 2, p % 2
    other = k * 2 + 1 - core

    def obs_peer(d):
        return lax.rem(o + d, obs_size)

    def obs_source(d):
        return lax.rem(o + obs_size - d, obs_size)

    def device(obs, par):
        return {"obs": obs, "par": par}

    def epochs_of(obs):
        return pl.ds(pl.multiple_of(obs * epochs, epochs), epochs)

    def lanes_of(which, g, offset=0):
        return pl.ds(pl.multiple_of(offset + which * half + g * width, LANES), width)

    barrier = pltpu.get_barrier_semaphore()
    for d in range(1, obs_size):
        pl.semaphore_signal(barrier, inc=1, device_id=device(obs_peer(d), p), device_id_type=MESH)
    pl.semaphore_signal(barrier, inc=1, device_id=device(o, other), device_id_type=MESH)

    @pl.when(k < hops)
    def _():
        pl.semaphore_signal(barrier, inc=1, device_id=device(o, p + 2), device_id_type=MESH)

    @pl.when(k > 0)
    def _():
        pl.semaphore_signal(barrier, inc=1, device_id=device(o, p - 2), device_id_type=MESH)

    target = lax.broadcasted_iota(jnp.int32, (rows, rows), 0)
    source = lax.broadcasted_iota(jnp.int32, (rows, rows), 1)
    wanted = target * arcs
    for a in range(1, arcs):
        wanted = jnp.where(target >= a * epochs, (target - a * epochs) * arcs + a, wanted)
    sort = jnp.where(source == wanted, 1.0, 0.0).astype(jnp.bfloat16)
    for lo in range(0, columns, 512):
        size = min(512, columns - lo)
        tile = jnp.dot(sort, design_ref[:, lo : lo + size], preferred_element_type=jnp.float32)
        tile = tile.astype(jnp.bfloat16)
        for a in range(arcs):
            raw_ref[a, epochs_of(o), lo : lo + size] = tile[a * epochs : (a + 1) * epochs]

    near = jnp.where(k < hops, 1, 0) + jnp.where(k > 0, 1, 0)
    pl.semaphore_wait(barrier, obs_size + near)

    sent = []

    def place(g):
        return pltpu.make_async_copy(
            raw_ref.at[:, epochs_of(o), lanes_of(core, g)], pools[g].at[p], place_sem.at[g]
        )

    def across(g):
        return pltpu.make_async_remote_copy(
            raw_ref.at[:, epochs_of(o), lanes_of(1 - core, g)], pools[g].at[p],
            across_s.at[g], across_r.at[g], device_id=device(o, other), device_id_type=MESH,
        )

    def across_in(g):
        return pltpu.make_async_remote_copy(
            pools[g].at[other], pools[g].at[other],
            across_s.at[g], across_r.at[g], device_id=device(o, other), device_id_type=MESH,
        )

    def line(g, way, s, incoming):
        if way == 0:
            pair, to = (k - 1 - s if incoming else k - s), p + 2
        else:
            pair, to = (k + 1 + s if incoming else k + s), p - 2
        window = pools[g].at[pl.ds(pair * 2, 2)]
        return pltpu.make_async_remote_copy(
            window, window, line_s.at[way, g, s], line_r.at[way, g, s],
            device_id=device(o, to), device_id_type=MESH,
        )

    def sends(way, s):
        return ((k >= s) & (k < hops)) if way == 0 else ((k + s < chips) & (k > 0))

    def receives(way, s):
        return (k - 1 - s >= 0) if way == 0 else (k + 1 + s < chips)

    def line_wait(g, s):
        for way in (0, 1):
            @pl.when(receives(way, s))
            def _():
                line(g, way, s, True).wait_recv()

    def line_send(g, s):
        for way in (0, 1):
            @pl.when(sends(way, s))
            def _():
                line(g, way, s, False).start()

    def own_copy(d, owner):
        window = raw_ref.at[:, epochs_of(owner), :]
        return pltpu.make_async_remote_copy(
            window, window, own_s.at[d - 1], own_r.at[d - 1],
            device_id=device(obs_peer(d), p), device_id_type=MESH,
        )

    def swap(g, d, owner):
        return pltpu.make_async_remote_copy(
            stage_ref.at[g, d - 1], mixed_ref.at[g, :, epochs_of(owner), :],
            swap_s.at[g, d - 1], swap_r.at[g, d - 1],
            device_id=device(obs_peer(d), p), device_id_type=MESH,
        )

    def back(g, j, which):
        window = part_ref.at[:, :, lanes_of(which, g, j * columns)]
        return pltpu.make_async_remote_copy(
            window, window, back_s.at[g, j], back_r.at[g, j],
            device_id=device(o, other), device_id_type=MESH,
        )

    for g in range(chunks):
        place(g).start()
        across(g).start()
        sent.append(across(g))

    def first_send(g):
        place(g).wait()
        across_in(g).wait_recv()
        line_send(g, 0)

    first_send(0)
    for d in range(1, obs_size):
        own_copy(d, o).start()
        sent.append(own_copy(d, o))
    if chunks > 1:
        first_send(1)
    build_filters(taps_ref, limit_ref, filt_ref)

    for stage in range(1, chunks + hops):
        for s in range(1, hops):
            g = stage - s
            if 0 <= g < chunks:
                line_wait(g, s - 1)
                line_send(g, s)
        if stage + 1 < chunks:
            first_send(stage + 1)
        g = stage - hops
        if 0 <= g < chunks:
            line_wait(g, hops - 1)
            for d in range(1, obs_size):
                for j in range(blocks_per):
                    block = order_ref[obs_peer(d) * blocks_per + j]
                    stage_ref[g, d - 1, :, :, j * width : (j + 1) * width] = pools[g][block]
                swap(g, d, o).start()
                sent.append(swap(g, d, o))
            for j in range(blocks_per):
                block = order_ref[o * blocks_per + j]
                mixed_ref[g, :, epochs_of(o), j * width : (j + 1) * width] = pools[g][block]

    for d in range(1, obs_size):
        own_copy(d, obs_source(d)).wait_recv()
    tile_width = 256 if columns % 256 == 0 else LANES

    @pl.loop(0, columns // tile_width)
    def _(i):
        lanes = pl.ds(pl.multiple_of(i * tile_width, tile_width), tile_width)
        for a in range(arcs):
            own_ref[a, :, lanes] = jnp.dot(
                filt_ref[a], raw_ref[a, :, lanes], preferred_element_type=jnp.float32
            ).astype(jnp.bfloat16)

    for g in range(chunks):
        for d in range(1, obs_size):
            swap(g, d, obs_source(d)).wait_recv()
        for a in range(arcs):
            value = jnp.dot(filt_ref[a], mixed_ref[g, a], preferred_element_type=jnp.float32)
            value = value.astype(jnp.bfloat16)
            for j in range(blocks_per):
                part_ref[a, :, lanes_of(core, g, j * columns)] = value[:, j * width : (j + 1) * width]
        for j in range(blocks_per):
            back(g, j, core).start()
            sent.append(back(g, j, core))

    for g in range(chunks):
        for j in range(blocks_per):
            back(g, j, 1 - core).wait_recv()
    for copy in sent:
        copy.wait_send()
    for g in range(chunks):
        for s in range(hops):
            for way in (0, 1):
                @pl.when(sends(way, s))
                def _():
                    line(g, way, s, False).wait_send()


def per_device(obs_size, par_size, design, filter_taps, band_limit, col_order):
    rows, columns = design.shape
    arcs, arc_len = filter_taps.shape
    epochs = rows // arcs
    blocks_per = par_size // obs_size
    width = LANES
    chunks = columns // 2 // width
    hops = par_size // 2 - 1
    low = jnp.bfloat16
    vmem, smem = pl.BlockSpec(memory_space=pltpu.VMEM), pl.BlockSpec(memory_space=pltpu.SMEM)
    dma = pltpu.SemaphoreType.DMA
    own, part = pl.pallas_call(
        functools.partial(gather_kernel, obs_size, par_size, width),
        out_shape=(
            jax.ShapeDtypeStruct((arcs, arc_len, columns), low),
            jax.ShapeDtypeStruct((arcs, arc_len, blocks_per * columns), low),
        ),
        in_specs=[vmem, vmem, smem, smem],
        out_specs=(vmem, vmem),
        scratch_shapes=[
            pltpu.VMEM((arcs, arc_len, columns), low),
            pltpu.VMEM((arcs, arc_len, arc_len), low),
            pltpu.VMEM((chunks, obs_size - 1, arcs, epochs, blocks_per * width), low),
            pltpu.VMEM((chunks, arcs, arc_len, blocks_per * width), low),
            dma((chunks,)), dma((chunks,)), dma((chunks,)),
            dma((2, chunks, hops)), dma((2, chunks, hops)),
            dma((obs_size - 1,)), dma((obs_size - 1,)),
            dma((chunks, obs_size - 1)), dma((chunks, obs_size - 1)),
            dma((chunks, blocks_per)), dma((chunks, blocks_per)),
        ]
        + [pltpu.VMEM((par_size, arcs, epochs, width), low) for _ in range(chunks)],
        compiler_params=pltpu.CompilerParams(
            collective_id=0, has_side_effects=True, vmem_limit_bytes=56 * 1024 * 1024
        ),
    )(design, filter_taps, band_limit, col_order)
    total = arcs * arc_len
    product = lax.dot_general(
        own.reshape(total, columns), part.reshape(total, blocks_per * columns),
        (((0,), (0,)), ((), ())), preferred_element_type=jnp.float32,
    )
    return product / total


def solution(mesh):
    body = functools.partial(per_device, mesh.shape["obs"], mesh.shape["par"])
    placed = (P("obs", "par"), P(), P(), P())
    return jax.shard_map(body, mesh=mesh, in_specs=placed, out_specs=P("par", "obs"), check_vma=False)
```

```python
import functools

import jax
import jax.numpy as jnp
from jax import lax
from jax.experimental import pallas as pl
from jax.experimental.pallas import tpu as pltpu
from jax.sharding import PartitionSpec as P

MESH = pl.DeviceIdType.MESH
LANES = 128


def build_filters(taps_ref, limit_ref, filt_ref):
    arcs, arc_len = taps_ref.shape
    tiles = arc_len // LANES
    row = lax.broadcasted_iota(jnp.int32, (LANES, 2 * LANES), 0)
    upper = lax.broadcasted_iota(jnp.int32, (LANES, LANES), 1) >= lax.broadcasted_iota(
        jnp.int32, (LANES, LANES), 0
    )
    lag = lax.broadcasted_iota(jnp.int32, (1, arc_len), 1)
    for a in range(arcs):
        taps = taps_ref[a : a + 1, :].astype(jnp.bfloat16).astype(jnp.float32)
        taps = jnp.where(lag < limit_ref[a], taps, 0.0)
        for d in range(tiles):
            before = taps[:, (d - 1) * LANES : d * LANES] if d else jnp.zeros((1, LANES), jnp.float32)
            strip = jnp.concatenate([before, taps[:, d * LANES : (d + 1) * LANES]], axis=1)
            strip = jnp.broadcast_to(strip, (LANES, 2 * LANES))
            step = 1
            while step < LANES:
                strip = jnp.where((row & step) != 0, pltpu.roll(strip, step, 1), strip)
                step *= 2
            tile = strip[:, LANES:]
            mirrored = tile.T
            if d == 0:
                tile = jnp.where(upper, tile, mirrored)
            tile_low, mirrored_low = tile.astype(jnp.bfloat16), mirrored.astype(jnp.bfloat16)
            for i in range(tiles - d):
                lo, hi = pl.ds(i * LANES, LANES), pl.ds((i + d) * LANES, LANES)
                filt_ref[a, lo, hi] = tile_low
                if d:
                    filt_ref[a, hi, lo] = mirrored_low


def gather_kernel(
    obs_size, par_size, width, early,
    design_ref, taps_ref, limit_ref, order_ref,
    own_ref, part_ref, early_ref,
    raw_ref, filt_ref, stage_ref, mixed_ref,
    place_sem, across_s, across_r, line_s, line_r,
    own_s, own_r, swap_s, swap_r, back_s, back_r,
    *pools,
):
    arcs, arc_len, columns = raw_ref.shape
    rows = design_ref.shape[0]
    epochs = rows // arcs
    chunks = columns // (2 * width)
    total = arcs * arc_len
    blocks_per = par_size // obs_size
    chips = par_size // 2
    hops = chips - 1
    o, p = lax.axis_index("obs"), lax.axis_index("par")
    k, core = p // 2, p % 2
    other = k * 2 + 1 - core

    def obs_peer(d):
        return lax.rem(o + d, obs_size)

    def obs_source(d):
        return lax.rem(o + obs_size - d, obs_size)

    def device(obs, par):
        return {"obs": obs, "par": par}

    def epochs_of(obs):
        return pl.ds(pl.multiple_of(obs * epochs, epochs), epochs)

    def lanes_of(which, g=0):
        return pl.ds(pl.multiple_of((2 * g + which) * width, LANES), width)

    barrier = pltpu.get_barrier_semaphore()
    for d in range(1, obs_size):
        pl.semaphore_signal(barrier, inc=1, device_id=device(obs_peer(d), p), device_id_type=MESH)
    pl.semaphore_signal(barrier, inc=1, device_id=device(o, other), device_id_type=MESH)

    @pl.when(k < hops)
    def _():
        pl.semaphore_signal(barrier, inc=1, device_id=device(o, p + 2), device_id_type=MESH)

    @pl.when(k > 0)
    def _():
        pl.semaphore_signal(barrier, inc=1, device_id=device(o, p - 2), device_id_type=MESH)

    target = lax.broadcasted_iota(jnp.int32, (rows, rows), 0)
    source = lax.broadcasted_iota(jnp.int32, (rows, rows), 1)
    wanted = target * arcs
    for a in range(1, arcs):
        wanted = jnp.where(target >= a * epochs, (target - a * epochs) * arcs + a, wanted)
    sort = jnp.where(source == wanted, 1.0, 0.0).astype(jnp.bfloat16)
    for lo in range(0, columns, 512):
        size = min(512, columns - lo)
        tile = jnp.dot(sort, design_ref[:, lo : lo + size], preferred_element_type=jnp.float32)
        tile = tile.astype(jnp.bfloat16)
        for a in range(arcs):
            raw_ref[a, epochs_of(o), lo : lo + size] = tile[a * epochs : (a + 1) * epochs]

    near = jnp.where(k < hops, 1, 0) + jnp.where(k > 0, 1, 0)
    pl.semaphore_wait(barrier, obs_size + near)

    sent = []

    def place(g):
        return pltpu.make_async_copy(
            raw_ref.at[:, epochs_of(o), lanes_of(core, g)], pools[g].at[p], place_sem.at[g]
        )

    def across(g):
        return pltpu.make_async_remote_copy(
            raw_ref.at[:, epochs_of(o), lanes_of(1 - core, g)], pools[g].at[p],
            across_s.at[g], across_r.at[g], device_id=device(o, other), device_id_type=MESH,
        )

    def across_in(g):
        return pltpu.make_async_remote_copy(
            pools[g].at[other], pools[g].at[other],
            across_s.at[g], across_r.at[g], device_id=device(o, other), device_id_type=MESH,
        )

    def line(g, way, s, incoming):
        if way == 0:
            pair, to = (k - 1 - s if incoming else k - s), p + 2
        else:
            pair, to = (k + 1 + s if incoming else k + s), p - 2
        window = pools[g].at[pl.ds(pair * 2, 2)]
        return pltpu.make_async_remote_copy(
            window, window, line_s.at[way, g, s], line_r.at[way, g, s],
            device_id=device(o, to), device_id_type=MESH,
        )

    def sends(way, s):
        return ((k >= s) & (k < hops)) if way == 0 else ((k + s < chips) & (k > 0))

    def receives(way, s):
        return (k - 1 - s >= 0) if way == 0 else (k + 1 + s < chips)

    def line_wait(g, s):
        for way in (0, 1):
            @pl.when(receives(way, s))
            def _():
                line(g, way, s, True).wait_recv()

    def line_send(g, s):
        for way in (0, 1):
            @pl.when(sends(way, s))
            def _():
                line(g, way, s, False).start()

    square = obs_size == 4 and arcs == 2
    first = lax.rem(o, 2)
    beside = (o - first + 1 - first, 2 - o + 2 * first)

    def own_copy(d, owner):
        window = raw_ref.at[:, epochs_of(owner), :]
        return pltpu.make_async_remote_copy(
            window, window, own_s.at[d - 1], own_r.at[d - 1],
            device_id=device(obs_peer(d), p), device_id_type=MESH,
        )

    def own_arc(way, a, owner, slot):
        window = raw_ref.at[a, epochs_of(owner), :]
        return pltpu.make_async_remote_copy(
            window, window, own_s.at[slot], own_r.at[slot],
            device_id=device(beside[way], p), device_id_type=MESH,
        )

    def own_send():
        if square:
            for a in range(arcs):
                for way in range(2):
                    copy = own_arc(way, (a + way) % 2, o, 3 * way + a)
                    copy.start()
                    sent.append(copy)
        else:
            for d in range(1, obs_size):
                own_copy(d, o).start()
                sent.append(own_copy(d, o))

    def own_forward():
        if square:
            for way in range(2):
                own_arc(way, way, beside[way], 3 * way).wait_recv()
            for way in range(2):
                copy = own_arc(1 - way, way, beside[way], 3 * (1 - way) + 2)
                copy.start()
                sent.append(copy)

    def own_wait():
        if square:
            for way in range(2):
                own_arc(way, 1 - way, beside[way], 3 * way + 1).wait_recv()
                own_arc(way, 1 - way, 3 - o, 3 * way + 2).wait_recv()
        else:
            for d in range(1, obs_size):
                own_copy(d, obs_source(d)).wait_recv()

    def swap(g, d, owner):
        return pltpu.make_async_remote_copy(
            stage_ref.at[g, d - 1], mixed_ref.at[g, :, epochs_of(owner), :],
            swap_s.at[g, d - 1], swap_r.at[g, d - 1],
            device_id=device(obs_peer(d), p), device_id_type=MESH,
        )

    def back(g, which):
        window = part_ref.at[g, :, :, lanes_of(which)]
        return pltpu.make_async_remote_copy(
            window, window, back_s.at[g], back_r.at[g],
            device_id=device(o, other), device_id_type=MESH,
        )

    def filter_own():
        own_wait()
        size = 2 * width

        @pl.loop(0, columns // size)
        def _(i):
            lanes = pl.ds(pl.multiple_of(i * size, size), size)
            for a in range(arcs):
                value = jnp.dot(filt_ref[a], raw_ref[a, :, lanes], preferred_element_type=jnp.float32)
                own_ref[lanes, a * arc_len : (a + 1) * arc_len] = value.T.astype(jnp.bfloat16)

    def filter_chunk(g):
        for d in range(1, obs_size):
            swap(g, d, obs_source(d)).wait_recv()
        for a in range(arcs):
            value = jnp.dot(filt_ref[a], mixed_ref[g, a], preferred_element_type=jnp.float32)
            value = value.astype(jnp.bfloat16)
            for j in range(blocks_per):
                part_ref[g, j, a * arc_len : (a + 1) * arc_len, lanes_of(core)] = (
                    value[:, j * width : (j + 1) * width]
                )
        back(g, core).start()
        sent.append(back(g, core))

    def early_product(g):
        back(g, 1 - core).wait_recv()
        for j in range(blocks_per):
            @pl.loop(0, columns // 256)
            def _(i):
                here = pl.ds(pl.multiple_of(i * 256, 256), 256)
                value = jnp.dot(own_ref[here, :], part_ref[g, j], preferred_element_type=jnp.float32)
                early_ref[g * blocks_per + j, here, :] = value * (1.0 / total)

    for g in range(chunks):
        place(g).start()
        across(g).start()
        sent.append(across(g))

    def first_send(g):
        place(g).wait()
        across_in(g).wait_recv()
        line_send(g, 0)

    first_send(0)
    own_send()
    if chunks > 1:
        first_send(1)
    build_filters(taps_ref, limit_ref, filt_ref)

    done = 0
    for stage in range(1, chunks + hops):
        for s in range(1, hops):
            g = stage - s
            if 0 <= g < chunks:
                line_wait(g, s - 1)
                line_send(g, s)
        if stage + 1 < chunks:
            first_send(stage + 1)
        g = stage - hops
        if 0 <= g < chunks:
            line_wait(g, hops - 1)
            if g == 0:
                own_forward()
            for d in range(1, obs_size):
                for j in range(blocks_per):
                    block = order_ref[obs_peer(d) * blocks_per + j]
                    stage_ref[g, d - 1, :, :, j * width : (j + 1) * width] = pools[g][block]
                swap(g, d, o).start()
                sent.append(swap(g, d, o))
            for j in range(blocks_per):
                block = order_ref[o * blocks_per + j]
                mixed_ref[g, :, epochs_of(o), j * width : (j + 1) * width] = pools[g][block]

        if stage == chunks + hops - 3:
            filter_own()
        if stage > chunks + hops - 3 and done < chunks - 1:
            filter_chunk(done)
            done += 1

    made = 0
    for g in range(done, chunks):
        filter_chunk(g)
        if made < early and g < chunks - 1:
            early_product(made)
            made += 1
    for g in range(made, early):
        early_product(g)
    for g in range(early, chunks):
        back(g, 1 - core).wait_recv()
    for copy in sent:
        copy.wait_send()
    for g in range(chunks):
        for s in range(hops):
            for way in (0, 1):
                @pl.when(sends(way, s))
                def _():
                    line(g, way, s, False).wait_send()


def product_kernel(early, own_ref, part_ref, early_ref, out_ref, tile_ref, tile_s, early_s):
    columns, total = own_ref.shape
    chunks, blocks_per, _, size = part_ref.shape
    late = (chunks - early) * blocks_per

    def early_copy(e):
        lanes = pl.ds((e % blocks_per) * columns + (e // blocks_per) * size, size)
        return pltpu.make_async_copy(early_ref.at[e], out_ref.at[:, lanes], early_s.at[e])

    def tile_copy(i, slot):
        start = (i % blocks_per) * columns + (early + i // blocks_per) * size
        lanes = pl.ds(pl.multiple_of(start, size), size)
        return pltpu.make_async_copy(tile_ref.at[slot], out_ref.at[:, lanes], tile_s.at[slot])

    for e in range(early * blocks_per):
        early_copy(e).start()

    @pl.loop(0, late)
    def _(i):
        slot = i % 2

        @pl.when(i >= 2)
        def _():
            tile_copy(i - 2, slot).wait()

        value = jnp.dot(
            own_ref[...], part_ref[early + i // blocks_per, i % blocks_per],
            preferred_element_type=jnp.float32,
        )
        tile_ref[slot] = value * (1.0 / total)
        tile_copy(i, slot).start()

    for i in range(max(late - 2, 0), late):
        tile_copy(i, i % 2).wait()
    for e in range(early * blocks_per):
        early_copy(e).wait()


def per_device(obs_size, par_size, design, filter_taps, band_limit, col_order):
    rows, columns = design.shape
    arcs, arc_len = filter_taps.shape
    epochs = rows // arcs
    total = arcs * arc_len
    blocks_per = par_size // obs_size
    width = LANES
    size = 2 * width
    chunks = columns // size
    hops = par_size // 2 - 1
    early = chunks // 2
    tiles = early * blocks_per
    low, full = jnp.bfloat16, jnp.float32
    vmem, smem = pl.BlockSpec(memory_space=pltpu.VMEM), pl.BlockSpec(memory_space=pltpu.SMEM)
    anywhere = pl.BlockSpec(memory_space=pl.ANY)
    dma = pltpu.SemaphoreType.DMA
    own, part, made = pl.pallas_call(
        functools.partial(gather_kernel, obs_size, par_size, width, early),
        out_shape=(
            pltpu.VMEM((columns, total), low),
            pltpu.VMEM((chunks, blocks_per, total, size), low),
            pltpu.VMEM((tiles, columns, size), full),
        ),
        in_specs=[vmem, vmem, smem, smem],
        out_specs=(vmem, vmem, vmem),
        scratch_shapes=[
            pltpu.VMEM((arcs, arc_len, columns), low),
            pltpu.VMEM((arcs, arc_len, arc_len), low),
            pltpu.VMEM((chunks, obs_size - 1, arcs, epochs, blocks_per * width), low),
            pltpu.VMEM((chunks, arcs, arc_len, blocks_per * width), low),
            dma((chunks,)), dma((chunks,)), dma((chunks,)),
            dma((2, chunks, hops)), dma((2, chunks, hops)),
            dma((max(6, obs_size),)), dma((max(6, obs_size),)),
            dma((chunks, obs_size - 1)), dma((chunks, obs_size - 1)),
            dma((chunks,)), dma((chunks,)),
        ]
        + [pltpu.VMEM((par_size, arcs, epochs, width), low) for _ in range(chunks)],
        compiler_params=pltpu.CompilerParams(
            collective_id=0, has_side_effects=True, vmem_limit_bytes=36 * 1024 * 1024
        ),
    )(design, filter_taps, band_limit, col_order)
    return pl.pallas_call(
        functools.partial(product_kernel, early),
        out_shape=jax.ShapeDtypeStruct((columns, blocks_per * columns), full),
        in_specs=[vmem, vmem, vmem],
        out_specs=anywhere,
        scratch_shapes=[pltpu.VMEM((2, columns, size), full), dma((2,)), dma((tiles,))],
        compiler_params=pltpu.CompilerParams(vmem_limit_bytes=24 * 1024 * 1024),
    )(own, part, made)


def solution(mesh):
    body = functools.partial(per_device, mesh.shape["obs"], mesh.shape["par"])
    placed = (P("obs", "par"), P(), P(), P())
    return jax.shard_map(body, mesh=mesh, in_specs=placed, out_specs=P("par", "obs"), check_vma=False)
```

```python
import functools

import jax
import jax.numpy as jnp
from jax import lax
from jax.experimental import pallas as pl
from jax.experimental.pallas import tpu as pltpu
from jax.sharding import PartitionSpec as P

MESH = pl.DeviceIdType.MESH
LANES = 128


def build_filters(taps_ref, limit_ref, filt_ref):
    arcs, arc_len = taps_ref.shape
    tiles = arc_len // LANES
    row = lax.broadcasted_iota(jnp.int32, (LANES, 2 * LANES), 0)
    upper = lax.broadcasted_iota(jnp.int32, (LANES, LANES), 1) >= lax.broadcasted_iota(
        jnp.int32, (LANES, LANES), 0
    )
    lag = lax.broadcasted_iota(jnp.int32, (1, arc_len), 1)
    for a in range(arcs):
        taps = taps_ref[a : a + 1, :].astype(jnp.bfloat16).astype(jnp.float32)
        taps = jnp.where(lag < limit_ref[a], taps, 0.0)
        for d in range(tiles):
            before = taps[:, (d - 1) * LANES : d * LANES] if d else jnp.zeros((1, LANES), jnp.float32)
            strip = jnp.concatenate([before, taps[:, d * LANES : (d + 1) * LANES]], axis=1)
            strip = jnp.broadcast_to(strip, (LANES, 2 * LANES))
            step = 1
            while step < LANES:
                strip = jnp.where((row & step) != 0, pltpu.roll(strip, step, 1), strip)
                step *= 2
            tile = strip[:, LANES:]
            mirrored = tile.T
            if d == 0:
                tile = jnp.where(upper, tile, mirrored)
            tile_low, mirrored_low = tile.astype(jnp.bfloat16), mirrored.astype(jnp.bfloat16)
            for i in range(tiles - d):
                lo, hi = pl.ds(i * LANES, LANES), pl.ds((i + d) * LANES, LANES)
                filt_ref[a, lo, hi] = tile_low
                if d:
                    filt_ref[a, hi, lo] = mirrored_low


def gather_kernel(
    obs_size, par_size, width, early,
    design_ref, taps_ref, limit_ref, order_ref,
    own_ref, part_ref, early_ref,
    raw_ref, filt_ref, stage_ref, mixed_ref,
    place_sem, across_s, across_r, line_s, line_r,
    own_s, own_r, swap_s, swap_r, back_s, back_r,
    *pools,
):
    arcs, arc_len, columns = raw_ref.shape
    rows = design_ref.shape[0]
    epochs = rows // arcs
    chunks = columns // (2 * width)
    total = arcs * arc_len
    blocks_per = par_size // obs_size
    chips = par_size // 2
    hops = chips - 1
    o, p = lax.axis_index("obs"), lax.axis_index("par")
    k, core = p // 2, p % 2
    other = k * 2 + 1 - core

    def obs_peer(d):
        return lax.rem(o + d, obs_size)

    def obs_source(d):
        return lax.rem(o + obs_size - d, obs_size)

    def device(obs, par):
        return {"obs": obs, "par": par}

    def epochs_of(obs):
        return pl.ds(pl.multiple_of(obs * epochs, epochs), epochs)

    def lanes_of(which, g=0):
        return pl.ds(pl.multiple_of((2 * g + which) * width, LANES), width)

    barrier = pltpu.get_barrier_semaphore()
    for d in range(1, obs_size):
        pl.semaphore_signal(barrier, inc=1, device_id=device(obs_peer(d), p), device_id_type=MESH)
    pl.semaphore_signal(barrier, inc=1, device_id=device(o, other), device_id_type=MESH)

    @pl.when(k < hops)
    def _():
        pl.semaphore_signal(barrier, inc=1, device_id=device(o, p + 2), device_id_type=MESH)

    @pl.when(k > 0)
    def _():
        pl.semaphore_signal(barrier, inc=1, device_id=device(o, p - 2), device_id_type=MESH)

    target = lax.broadcasted_iota(jnp.int32, (rows, rows), 0)
    source = lax.broadcasted_iota(jnp.int32, (rows, rows), 1)
    wanted = target * arcs
    for a in range(1, arcs):
        wanted = jnp.where(target >= a * epochs, (target - a * epochs) * arcs + a, wanted)
    sort = jnp.where(source == wanted, 1.0, 0.0).astype(jnp.bfloat16)
    for lo in range(0, columns, 512):
        size = min(512, columns - lo)
        tile = jnp.dot(sort, design_ref[:, lo : lo + size], preferred_element_type=jnp.float32)
        tile = tile.astype(jnp.bfloat16)
        for a in range(arcs):
            raw_ref[a, epochs_of(o), lo : lo + size] = tile[a * epochs : (a + 1) * epochs]

    near = jnp.where(k < hops, 1, 0) + jnp.where(k > 0, 1, 0)
    pl.semaphore_wait(barrier, obs_size + near)

    sent = []

    def place(g):
        return pltpu.make_async_copy(
            raw_ref.at[:, epochs_of(o), lanes_of(core, g)], pools[g].at[p], place_sem.at[g]
        )

    def across(g):
        return pltpu.make_async_remote_copy(
            raw_ref.at[:, epochs_of(o), lanes_of(1 - core, g)], pools[g].at[p],
            across_s.at[g], across_r.at[g], device_id=device(o, other), device_id_type=MESH,
        )

    def across_in(g):
        return pltpu.make_async_remote_copy(
            pools[g].at[other], pools[g].at[other],
            across_s.at[g], across_r.at[g], device_id=device(o, other), device_id_type=MESH,
        )

    def line(g, way, s, incoming):
        if way == 0:
            pair, to = (k - 1 - s if incoming else k - s), p + 2
        else:
            pair, to = (k + 1 + s if incoming else k + s), p - 2
        window = pools[g].at[pl.ds(pair * 2, 2)]
        return pltpu.make_async_remote_copy(
            window, window, line_s.at[way, g, s], line_r.at[way, g, s],
            device_id=device(o, to), device_id_type=MESH,
        )

    def sends(way, s):
        return ((k >= s) & (k < hops)) if way == 0 else ((k + s < chips) & (k > 0))

    def receives(way, s):
        return (k - 1 - s >= 0) if way == 0 else (k + 1 + s < chips)

    def line_wait(g, s):
        for way in (0, 1):
            @pl.when(receives(way, s))
            def _():
                line(g, way, s, True).wait_recv()

    def line_send(g, s):
        for way in (0, 1):
            @pl.when(sends(way, s))
            def _():
                line(g, way, s, False).start()

    square = obs_size == 4 and arcs == 2
    first = lax.rem(o, 2)
    beside = (o - first + 1 - first, 2 - o + 2 * first)

    def own_copy(d, owner):
        window = raw_ref.at[:, epochs_of(owner), :]
        return pltpu.make_async_remote_copy(
            window, window, own_s.at[d - 1], own_r.at[d - 1],
            device_id=device(obs_peer(d), p), device_id_type=MESH,
        )

    def own_arc(way, a, owner, slot):
        window = raw_ref.at[a, epochs_of(owner), :]
        return pltpu.make_async_remote_copy(
            window, window, own_s.at[slot], own_r.at[slot],
            device_id=device(beside[way], p), device_id_type=MESH,
        )

    def own_send():
        if square:
            for a in range(arcs):
                for way in range(2):
                    copy = own_arc(way, (a + way) % 2, o, 3 * way + a)
                    copy.start()
                    sent.append(copy)
        else:
            for d in range(1, obs_size):
                own_copy(d, o).start()
                sent.append(own_copy(d, o))

    def own_forward():
        if square:
            for way in range(2):
                own_arc(way, way, beside[way], 3 * way).wait_recv()
            for way in range(2):
                copy = own_arc(1 - way, way, beside[way], 3 * (1 - way) + 2)
                copy.start()
                sent.append(copy)

    def own_wait():
        if square:
            for way in range(2):
                own_arc(way, 1 - way, beside[way], 3 * way + 1).wait_recv()
                own_arc(way, 1 - way, 3 - o, 3 * way + 2).wait_recv()
        else:
            for d in range(1, obs_size):
                own_copy(d, obs_source(d)).wait_recv()

    def swap(g, d, owner):
        return pltpu.make_async_remote_copy(
            stage_ref.at[g, d - 1], mixed_ref.at[g, :, epochs_of(owner), :],
            swap_s.at[g, d - 1], swap_r.at[g, d - 1],
            device_id=device(obs_peer(d), p), device_id_type=MESH,
        )

    def back(g, which):
        window = part_ref.at[g, :, :, lanes_of(which)]
        return pltpu.make_async_remote_copy(
            window, window, back_s.at[g], back_r.at[g],
            device_id=device(o, other), device_id_type=MESH,
        )

    def filter_own(begin, end):
        size = 2 * width

        @pl.loop(begin, end)
        def _(i):
            lanes = pl.ds(pl.multiple_of(i * size, size), size)
            for a in range(arcs):
                value = jnp.dot(filt_ref[a], raw_ref[a, :, lanes], preferred_element_type=jnp.float32)
                own_ref[lanes, a * arc_len : (a + 1) * arc_len] = value.T.astype(jnp.bfloat16)

    def filter_chunk(g):
        for d in range(1, obs_size):
            swap(g, d, obs_source(d)).wait_recv()
        for a in range(arcs):
            value = jnp.dot(filt_ref[a], mixed_ref[g, a], preferred_element_type=jnp.float32)
            value = value.astype(jnp.bfloat16)
            for j in range(blocks_per):
                part_ref[g, j, a * arc_len : (a + 1) * arc_len, lanes_of(core)] = (
                    value[:, j * width : (j + 1) * width]
                )
        back(g, core).start()
        sent.append(back(g, core))

    def early_product(g):
        back(g, 1 - core).wait_recv()
        for j in range(blocks_per):
            @pl.loop(0, columns // 256)
            def _(i):
                here = pl.ds(pl.multiple_of(i * 256, 256), 256)
                value = jnp.dot(own_ref[here, :], part_ref[g, j], preferred_element_type=jnp.float32)
                early_ref[j, here, g * 256 : (g + 1) * 256] = value * (1.0 / total)

    for g in range(chunks):
        place(g).start()
        across(g).start()
        sent.append(across(g))

    def first_send(g):
        place(g).wait()
        across_in(g).wait_recv()
        line_send(g, 0)

    own_send()
    for g in range(min(3, chunks)):
        first_send(g)
    build_filters(taps_ref, limit_ref, filt_ref)

    for stage in range(1, chunks + hops):
        for s in range(1, hops):
            g = stage - s
            if 0 <= g < chunks:
                line_wait(g, s - 1)
                line_send(g, s)
        if stage + 2 < chunks:
            first_send(stage + 2)
        g = stage - hops
        if 0 <= g < chunks:
            line_wait(g, hops - 1)
            if g == 0:
                own_forward()
            for d in range(1, obs_size):
                for j in range(blocks_per):
                    block = order_ref[obs_peer(d) * blocks_per + j]
                    stage_ref[g, d - 1, :, :, j * width : (j + 1) * width] = pools[g][block]
                swap(g, d, o).start()
                sent.append(swap(g, d, o))
            for j in range(blocks_per):
                block = order_ref[o * blocks_per + j]
                mixed_ref[g, :, epochs_of(o), j * width : (j + 1) * width] = pools[g][block]

        left = chunks + hops - 1 - stage
        if left < 4:
            if left == 3:
                own_wait()
            filter_own(chunks * (3 - left) // 4, chunks * (4 - left) // 4)

    made = 0
    for g in range(chunks):
        filter_chunk(g)
        if made < early and g < chunks - 1:
            early_product(made)
            made += 1
    for g in range(made, early):
        early_product(g)
    for g in range(early, chunks):
        back(g, 1 - core).wait_recv()
    for copy in sent:
        copy.wait_send()
    for g in range(chunks):
        for s in range(hops):
            for way in (0, 1):
                @pl.when(sends(way, s))
                def _():
                    line(g, way, s, False).wait_send()


def product_kernel(early, own_ref, part_ref, early_ref, out_ref, late_ref, early_s, late_s):
    columns, total = own_ref.shape
    chunks, blocks_per, _, size = part_ref.shape
    split = early * size
    rest = columns - split
    bands = late_s.shape[0]
    rows = columns // bands

    def early_copy(j):
        lanes = pl.ds(j * columns, split)
        return pltpu.make_async_copy(early_ref.at[j], out_ref.at[:, lanes], early_s.at[j])

    def late_copy(i, j):
        here = pl.ds(pl.multiple_of(i * rows, rows), rows)
        lanes = pl.ds(j * columns + split, rest)
        return pltpu.make_async_copy(late_ref.at[j, here, :], out_ref.at[here, lanes], late_s.at[i, j])

    for j in range(blocks_per):
        early_copy(j).start()

    @pl.loop(0, bands)
    def _(i):
        here = pl.ds(pl.multiple_of(i * rows, rows), rows)
        for j in range(blocks_per):
            for g in range(early, chunks):
                value = jnp.dot(own_ref[here, :], part_ref[g, j], preferred_element_type=jnp.float32)
                lo = (g - early) * size
                late_ref[j, here, lo : lo + size] = value * (1.0 / total)
            late_copy(i, j).start()

    for i in range(bands):
        for j in range(blocks_per):
            late_copy(i, j).wait()
    for j in range(blocks_per):
        early_copy(j).wait()


def per_device(obs_size, par_size, design, filter_taps, band_limit, col_order):
    rows, columns = design.shape
    arcs, arc_len = filter_taps.shape
    epochs = rows // arcs
    total = arcs * arc_len
    blocks_per = par_size // obs_size
    width = LANES
    size = 2 * width
    chunks = columns // size
    hops = par_size // 2 - 1
    early = chunks // 2
    split = early * size
    bands = 3
    low, full = jnp.bfloat16, jnp.float32
    vmem, smem = pl.BlockSpec(memory_space=pltpu.VMEM), pl.BlockSpec(memory_space=pltpu.SMEM)
    anywhere = pl.BlockSpec(memory_space=pl.ANY)
    dma = pltpu.SemaphoreType.DMA
    own, part, made = pl.pallas_call(
        functools.partial(gather_kernel, obs_size, par_size, width, early),
        out_shape=(
            pltpu.VMEM((columns, total), low),
            pltpu.VMEM((chunks, blocks_per, total, size), low),
            pltpu.VMEM((blocks_per, columns, split), full),
        ),
        in_specs=[vmem, vmem, smem, smem],
        out_specs=(vmem, vmem, vmem),
        scratch_shapes=[
            pltpu.VMEM((arcs, arc_len, columns), low),
            pltpu.VMEM((arcs, arc_len, arc_len), low),
            pltpu.VMEM((chunks, obs_size - 1, arcs, epochs, blocks_per * width), low),
            pltpu.VMEM((chunks, arcs, arc_len, blocks_per * width), low),
            dma((chunks,)), dma((chunks,)), dma((chunks,)),
            dma((2, chunks, hops)), dma((2, chunks, hops)),
            dma((max(6, obs_size),)), dma((max(6, obs_size),)),
            dma((chunks, obs_size - 1)), dma((chunks, obs_size - 1)),
            dma((chunks,)), dma((chunks,)),
        ]
        + [pltpu.VMEM((par_size, arcs, epochs, width), low) for _ in range(chunks)],
        compiler_params=pltpu.CompilerParams(
            collective_id=0, has_side_effects=True, vmem_limit_bytes=36 * 1024 * 1024
        ),
    )(design, filter_taps, band_limit, col_order)
    return pl.pallas_call(
        functools.partial(product_kernel, early),
        out_shape=jax.ShapeDtypeStruct((columns, blocks_per * columns), full),
        in_specs=[vmem, vmem, vmem],
        out_specs=anywhere,
        scratch_shapes=[
            pltpu.VMEM((blocks_per, columns, columns - split), full),
            dma((blocks_per,)), dma((bands, blocks_per)),
        ],
        compiler_params=pltpu.CompilerParams(vmem_limit_bytes=24 * 1024 * 1024),
    )(own, part, made)


def solution(mesh):
    body = functools.partial(per_device, mesh.shape["obs"], mesh.shape["par"])
    placed = (P("obs", "par"), P(), P(), P())
    return jax.shard_map(body, mesh=mesh, in_specs=placed, out_specs=P("par", "obs"), check_vma=False)
```

```python
import functools

import jax
import jax.numpy as jnp
from jax import lax
from jax.experimental import pallas as pl
from jax.experimental.pallas import tpu as pltpu
from jax.sharding import PartitionSpec as P

MESH = pl.DeviceIdType.MESH
LANES = 128


def build_filters(taps_ref, limit_ref, filt_ref):
    arcs, arc_len = taps_ref.shape
    tiles = arc_len // LANES
    row = lax.broadcasted_iota(jnp.int32, (LANES, 2 * LANES), 0)
    upper = lax.broadcasted_iota(jnp.int32, (LANES, LANES), 1) >= lax.broadcasted_iota(
        jnp.int32, (LANES, LANES), 0
    )
    lag = lax.broadcasted_iota(jnp.int32, (1, arc_len), 1)
    for a in range(arcs):
        taps = taps_ref[a : a + 1, :].astype(jnp.bfloat16).astype(jnp.float32)
        taps = jnp.where(lag < limit_ref[a], taps, 0.0)
        for d in range(tiles):
            before = taps[:, (d - 1) * LANES : d * LANES] if d else jnp.zeros((1, LANES), jnp.float32)
            strip = jnp.concatenate([before, taps[:, d * LANES : (d + 1) * LANES]], axis=1)
            strip = jnp.broadcast_to(strip, (LANES, 2 * LANES))
            step = 1
            while step < LANES:
                strip = jnp.where((row & step) != 0, pltpu.roll(strip, step, 1), strip)
                step *= 2
            tile = strip[:, LANES:]
            mirrored = tile.T
            if d == 0:
                tile = jnp.where(upper, tile, mirrored)
            tile_low, mirrored_low = tile.astype(jnp.bfloat16), mirrored.astype(jnp.bfloat16)
            for i in range(tiles - d):
                lo, hi = pl.ds(i * LANES, LANES), pl.ds((i + d) * LANES, LANES)
                filt_ref[a, lo, hi] = tile_low
                if d:
                    filt_ref[a, hi, lo] = mirrored_low


def gather_kernel(
    obs_size, par_size, width, early,
    design_ref, taps_ref, limit_ref, order_ref,
    own_ref, part_ref, early_ref,
    raw_ref, filt_ref, stage_ref, mixed_ref,
    place_sem, across_s, across_r, line_s, line_r,
    own_s, own_r, swap_s, swap_r, back_s, back_r,
    *pools,
):
    arcs, arc_len, columns = raw_ref.shape
    rows = design_ref.shape[0]
    epochs = rows // arcs
    chunks = columns // (2 * width)
    total = arcs * arc_len
    blocks_per = par_size // obs_size
    chips = par_size // 2
    hops = chips - 1
    o, p = lax.axis_index("obs"), lax.axis_index("par")
    k, core = p // 2, p % 2
    other = k * 2 + 1 - core

    def obs_peer(d):
        return lax.rem(o + d, obs_size)

    def obs_source(d):
        return lax.rem(o + obs_size - d, obs_size)

    def device(obs, par):
        return {"obs": obs, "par": par}

    def epochs_of(obs):
        return pl.ds(pl.multiple_of(obs * epochs, epochs), epochs)

    def lanes_of(which, g=0):
        return pl.ds(pl.multiple_of((2 * g + which) * width, LANES), width)

    barrier = pltpu.get_barrier_semaphore()
    for d in range(1, obs_size):
        pl.semaphore_signal(barrier, inc=1, device_id=device(obs_peer(d), p), device_id_type=MESH)
    pl.semaphore_signal(barrier, inc=1, device_id=device(o, other), device_id_type=MESH)

    @pl.when(k < hops)
    def _():
        pl.semaphore_signal(barrier, inc=1, device_id=device(o, p + 2), device_id_type=MESH)

    @pl.when(k > 0)
    def _():
        pl.semaphore_signal(barrier, inc=1, device_id=device(o, p - 2), device_id_type=MESH)

    target = lax.broadcasted_iota(jnp.int32, (rows, rows), 0)
    source = lax.broadcasted_iota(jnp.int32, (rows, rows), 1)
    wanted = target * arcs
    for a in range(1, arcs):
        wanted = jnp.where(target >= a * epochs, (target - a * epochs) * arcs + a, wanted)
    sort = jnp.where(source == wanted, 1.0, 0.0).astype(jnp.bfloat16)
    for lo in range(0, columns, 512):
        size = min(512, columns - lo)
        tile = jnp.dot(sort, design_ref[:, lo : lo + size], preferred_element_type=jnp.float32)
        tile = tile.astype(jnp.bfloat16)
        for a in range(arcs):
            raw_ref[a, epochs_of(o), lo : lo + size] = tile[a * epochs : (a + 1) * epochs]

    near = jnp.where(k < hops, 1, 0) + jnp.where(k > 0, 1, 0)
    pl.semaphore_wait(barrier, obs_size + near)

    sent = []

    def place(g):
        return pltpu.make_async_copy(
            raw_ref.at[:, epochs_of(o), lanes_of(core, g)], pools[g].at[p], place_sem.at[g]
        )

    def across(g):
        return pltpu.make_async_remote_copy(
            raw_ref.at[:, epochs_of(o), lanes_of(1 - core, g)], pools[g].at[p],
            across_s.at[g], across_r.at[g], device_id=device(o, other), device_id_type=MESH,
        )

    def across_in(g):
        return pltpu.make_async_remote_copy(
            pools[g].at[other], pools[g].at[other],
            across_s.at[g], across_r.at[g], device_id=device(o, other), device_id_type=MESH,
        )

    def line(g, way, s, incoming):
        if way == 0:
            pair, to = (k - 1 - s if incoming else k - s), p + 2
        else:
            pair, to = (k + 1 + s if incoming else k + s), p - 2
        window = pools[g].at[pl.ds(pair * 2, 2)]
        return pltpu.make_async_remote_copy(
            window, window, line_s.at[way, g, s], line_r.at[way, g, s],
            device_id=device(o, to), device_id_type=MESH,
        )

    def ahead(s):
        return 2 if s == 0 else 1

    def sends(way, s):
        return ((k >= s) & (k < hops)) if way == 0 else ((k + s < chips) & (k > 0))

    def receives(way, s):
        return (k - 1 - s >= 0) if way == 0 else (k + 1 + s < chips)

    def line_wait(g, s):
        for way in (0, 1):
            @pl.when(receives(way, s))
            def _():
                line(g, way, s, True).wait_recv()

    def line_send(g, s):
        for way in (0, 1):
            @pl.when(sends(way, s))
            def _():
                if g >= ahead(s):
                    line(g - ahead(s), way, s, False).wait_send()
                line(g, way, s, False).start()

    square = obs_size == 4 and arcs == 2
    first = lax.rem(o, 2)
    beside = (o - first + 1 - first, 2 - o + 2 * first)

    def own_copy(d, owner):
        window = raw_ref.at[:, epochs_of(owner), :]
        return pltpu.make_async_remote_copy(
            window, window, own_s.at[d - 1], own_r.at[d - 1],
            device_id=device(obs_peer(d), p), device_id_type=MESH,
        )

    def own_arc(way, a, owner, slot):
        window = raw_ref.at[a, epochs_of(owner), :]
        return pltpu.make_async_remote_copy(
            window, window, own_s.at[slot], own_r.at[slot],
            device_id=device(beside[way], p), device_id_type=MESH,
        )

    def own_send(a):
        if square:
            for way in range(2):
                copy = own_arc(way, (a + way) % 2, o, 3 * way + a)
                copy.start()
                sent.append(copy)
        elif a == 0:
            for d in range(1, obs_size):
                own_copy(d, o).start()
                sent.append(own_copy(d, o))

    def own_forward():
        if square:
            for way in range(2):
                own_arc(way, way, beside[way], 3 * way).wait_recv()
            for way in range(2):
                copy = own_arc(1 - way, way, beside[way], 3 * (1 - way) + 2)
                copy.start()
                sent.append(copy)

    def own_wait():
        if square:
            for way in range(2):
                own_arc(way, 1 - way, beside[way], 3 * way + 1).wait_recv()
                own_arc(way, 1 - way, 3 - o, 3 * way + 2).wait_recv()
        else:
            for d in range(1, obs_size):
                own_copy(d, obs_source(d)).wait_recv()

    def swap(g, d, owner):
        return pltpu.make_async_remote_copy(
            stage_ref.at[g, d - 1], mixed_ref.at[g, :, epochs_of(owner), :],
            swap_s.at[g, d - 1], swap_r.at[g, d - 1],
            device_id=device(obs_peer(d), p), device_id_type=MESH,
        )

    def back(g, which):
        window = part_ref.at[g, :, :, lanes_of(which)]
        return pltpu.make_async_remote_copy(
            window, window, back_s.at[g], back_r.at[g],
            device_id=device(o, other), device_id_type=MESH,
        )

    def filter_own(begin, end):
        size = 2 * width

        @pl.loop(begin, end)
        def _(i):
            lanes = pl.ds(pl.multiple_of(i * size, size), size)
            for a in range(arcs):
                value = jnp.dot(filt_ref[a], raw_ref[a, :, lanes], preferred_element_type=jnp.float32)
                own_ref[lanes, a * arc_len : (a + 1) * arc_len] = value.T.astype(jnp.bfloat16)

    def filter_chunk(g):
        for d in range(1, obs_size):
            swap(g, d, obs_source(d)).wait_recv()
        for a in range(arcs):
            value = jnp.dot(filt_ref[a], mixed_ref[g, a], preferred_element_type=jnp.float32)
            value = value.astype(jnp.bfloat16)
            for j in range(blocks_per):
                part_ref[g, j, a * arc_len : (a + 1) * arc_len, lanes_of(core)] = (
                    value[:, j * width : (j + 1) * width]
                )
        back(g, core).start()
        sent.append(back(g, core))

    def early_product(g):
        back(g, 1 - core).wait_recv()
        for j in range(blocks_per):
            @pl.loop(0, columns // 256)
            def _(i):
                here = pl.ds(pl.multiple_of(i * 256, 256), 256)
                value = jnp.dot(own_ref[here, :], part_ref[g, j], preferred_element_type=jnp.float32)
                early_ref[j, here, g * 256 : (g + 1) * 256] = value * (1.0 / total)

    for g in range(chunks):
        place(g).start()
        across(g).start()
        sent.append(across(g))

    def first_send(g):
        place(g).wait()
        across_in(g).wait_recv()
        line_send(g, 0)

    own_send(0)
    for g in range(min(2, chunks)):
        first_send(g)
    build_filters(taps_ref, limit_ref, filt_ref)

    done = 0
    for stage in range(1, chunks + hops):
        for s in range(1, hops):
            g = stage - s
            if 0 <= g < chunks:
                line_wait(g, s - 1)
                line_send(g, s)
        if stage + 1 < chunks:
            first_send(stage + 1)
        if stage == 1:
            own_send(1)
        g = stage - hops
        if 0 <= g < chunks:
            line_wait(g, hops - 1)
            if g == 0:
                own_forward()
            for d in range(1, obs_size):
                for j in range(blocks_per):
                    block = order_ref[obs_peer(d) * blocks_per + j]
                    stage_ref[g, d - 1, :, :, j * width : (j + 1) * width] = pools[g][block]
                swap(g, d, o).start()
                sent.append(swap(g, d, o))
            for j in range(blocks_per):
                block = order_ref[o * blocks_per + j]
                mixed_ref[g, :, epochs_of(o), j * width : (j + 1) * width] = pools[g][block]

        left = chunks + hops - 1 - stage
        if left < 3:
            if left == 2:
                own_wait()
            else:
                filter_chunk(done)
                done += 1
            filter_own(chunks * (2 - left) // 3, chunks * (3 - left) // 3)

    made = 0
    for g in range(done, chunks):
        filter_chunk(g)
        if made < early and g < chunks - 1:
            early_product(made)
            made += 1
    for g in range(made, early):
        early_product(g)
    for g in range(early, chunks):
        back(g, 1 - core).wait_recv()
    for copy in sent:
        copy.wait_send()
    for s in range(hops):
        for g in range(max(chunks - ahead(s), 0), chunks):
            for way in (0, 1):
                @pl.when(sends(way, s))
                def _():
                    line(g, way, s, False).wait_send()


def product_kernel(early, own_ref, part_ref, early_ref, out_ref, late_ref, early_s, late_s):
    columns, total = own_ref.shape
    chunks, blocks_per, _, size = part_ref.shape
    split = early * size
    rest = columns - split
    bands = late_s.shape[0]
    rows = columns // bands

    def early_copy(j):
        lanes = pl.ds(j * columns, split)
        return pltpu.make_async_copy(early_ref.at[j], out_ref.at[:, lanes], early_s.at[j])

    def late_copy(i, j):
        here = pl.ds(pl.multiple_of(i * rows, rows), rows)
        lanes = pl.ds(j * columns + split, rest)
        return pltpu.make_async_copy(late_ref.at[j, here, :], out_ref.at[here, lanes], late_s.at[i, j])

    for j in range(blocks_per):
        early_copy(j).start()

    @pl.loop(0, bands)
    def _(i):
        here = pl.ds(pl.multiple_of(i * rows, rows), rows)
        for j in range(blocks_per):
            for g in range(early, chunks):
                value = jnp.dot(own_ref[here, :], part_ref[g, j], preferred_element_type=jnp.float32)
                lo = (g - early) * size
                late_ref[j, here, lo : lo + size] = value * (1.0 / total)
            late_copy(i, j).start()

    for i in range(bands):
        for j in range(blocks_per):
            late_copy(i, j).wait()
    for j in range(blocks_per):
        early_copy(j).wait()


def per_device(obs_size, par_size, design, filter_taps, band_limit, col_order):
    rows, columns = design.shape
    arcs, arc_len = filter_taps.shape
    epochs = rows // arcs
    total = arcs * arc_len
    blocks_per = par_size // obs_size
    width = LANES
    size = 2 * width
    chunks = columns // size
    hops = par_size // 2 - 1
    early = chunks // 2
    split = early * size
    bands = 3
    low, full = jnp.bfloat16, jnp.float32
    vmem, smem = pl.BlockSpec(memory_space=pltpu.VMEM), pl.BlockSpec(memory_space=pltpu.SMEM)
    anywhere = pl.BlockSpec(memory_space=pl.ANY)
    dma = pltpu.SemaphoreType.DMA
    own, part, made = pl.pallas_call(
        functools.partial(gather_kernel, obs_size, par_size, width, early),
        out_shape=(
            pltpu.VMEM((columns, total), low),
            pltpu.VMEM((chunks, blocks_per, total, size), low),
            pltpu.VMEM((blocks_per, columns, split), full),
        ),
        in_specs=[vmem, vmem, smem, smem],
        out_specs=(vmem, vmem, vmem),
        scratch_shapes=[
            pltpu.VMEM((arcs, arc_len, columns), low),
            pltpu.VMEM((arcs, arc_len, arc_len), low),
            pltpu.VMEM((chunks, obs_size - 1, arcs, epochs, blocks_per * width), low),
            pltpu.VMEM((chunks, arcs, arc_len, blocks_per * width), low),
            dma((chunks,)), dma((chunks,)), dma((chunks,)),
            dma((2, chunks, hops)), dma((2, chunks, hops)),
            dma((max(6, obs_size),)), dma((max(6, obs_size),)),
            dma((chunks, obs_size - 1)), dma((chunks, obs_size - 1)),
            dma((chunks,)), dma((chunks,)),
        ]
        + [pltpu.VMEM((par_size, arcs, epochs, width), low) for _ in range(chunks)],
        compiler_params=pltpu.CompilerParams(
            collective_id=0, has_side_effects=True, vmem_limit_bytes=36 * 1024 * 1024
        ),
    )(design, filter_taps, band_limit, col_order)
    return pl.pallas_call(
        functools.partial(product_kernel, early),
        out_shape=jax.ShapeDtypeStruct((columns, blocks_per * columns), full),
        in_specs=[vmem, vmem, vmem],
        out_specs=anywhere,
        scratch_shapes=[
            pltpu.VMEM((blocks_per, columns, columns - split), full),
            dma((blocks_per,)), dma((bands, blocks_per)),
        ],
        compiler_params=pltpu.CompilerParams(vmem_limit_bytes=24 * 1024 * 1024),
    )(own, part, made)


def solution(mesh):
    body = functools.partial(per_device, mesh.shape["obs"], mesh.shape["par"])
    placed = (P("obs", "par"), P(), P(), P())
    return jax.shard_map(body, mesh=mesh, in_specs=placed, out_specs=P("par", "obs"), check_vma=False)
```

```python
import functools

import jax
import jax.numpy as jnp
from jax import lax
from jax.experimental import pallas as pl
from jax.experimental.pallas import tpu as pltpu
from jax.sharding import PartitionSpec as P

MESH = pl.DeviceIdType.MESH
LANES = 128


def build_filters(taps_ref, limit_ref, filt_ref):
    arcs, arc_len = taps_ref.shape
    tiles = arc_len // LANES
    row = lax.broadcasted_iota(jnp.int32, (LANES, 2 * LANES), 0)
    upper = lax.broadcasted_iota(jnp.int32, (LANES, LANES), 1) >= lax.broadcasted_iota(
        jnp.int32, (LANES, LANES), 0
    )
    lag = lax.broadcasted_iota(jnp.int32, (1, arc_len), 1)
    for a in range(arcs):
        taps = taps_ref[a : a + 1, :].astype(jnp.bfloat16).astype(jnp.float32)
        taps = jnp.where(lag < limit_ref[a], taps, 0.0)
        for d in range(tiles):
            before = taps[:, (d - 1) * LANES : d * LANES] if d else jnp.zeros((1, LANES), jnp.float32)
            strip = jnp.concatenate([before, taps[:, d * LANES : (d + 1) * LANES]], axis=1)
            strip = jnp.broadcast_to(strip, (LANES, 2 * LANES))
            step = 1
            while step < LANES:
                strip = jnp.where((row & step) != 0, pltpu.roll(strip, step, 1), strip)
                step *= 2
            tile = strip[:, LANES:]
            mirrored = tile.T
            if d == 0:
                tile = jnp.where(upper, tile, mirrored)
            tile_low, mirrored_low = tile.astype(jnp.bfloat16), mirrored.astype(jnp.bfloat16)
            for i in range(tiles - d):
                lo, hi = pl.ds(i * LANES, LANES), pl.ds((i + d) * LANES, LANES)
                filt_ref[a, lo, hi] = tile_low
                if d:
                    filt_ref[a, hi, lo] = mirrored_low


def gather_kernel(
    obs_size, par_size, width, early,
    design_ref, taps_ref, limit_ref, order_ref,
    own_ref, part_ref, early_ref,
    raw_ref, filt_ref, stage_ref, mixed_ref,
    place_sem, across_s, across_r, line_s, line_r,
    own_s, own_r, swap_s, swap_r, back_s, back_r,
    *pools,
):
    arcs, arc_len, columns = raw_ref.shape
    rows = design_ref.shape[0]
    epochs = rows // arcs
    chunks = columns // (2 * width)
    total = arcs * arc_len
    blocks_per = par_size // obs_size
    chips = par_size // 2
    hops = chips - 1
    o, p = lax.axis_index("obs"), lax.axis_index("par")
    k, core = p // 2, p % 2
    other = k * 2 + 1 - core

    def obs_peer(d):
        return lax.rem(o + d, obs_size)

    def obs_source(d):
        return lax.rem(o + obs_size - d, obs_size)

    def device(obs, par):
        return {"obs": obs, "par": par}

    def epochs_of(obs):
        return pl.ds(pl.multiple_of(obs * epochs, epochs), epochs)

    def lanes_of(which, g=0):
        return pl.ds(pl.multiple_of((2 * g + which) * width, LANES), width)

    barrier = pltpu.get_barrier_semaphore()
    for d in range(1, obs_size):
        pl.semaphore_signal(barrier, inc=1, device_id=device(obs_peer(d), p), device_id_type=MESH)
    pl.semaphore_signal(barrier, inc=1, device_id=device(o, other), device_id_type=MESH)

    @pl.when(k < hops)
    def _():
        pl.semaphore_signal(barrier, inc=1, device_id=device(o, p + 2), device_id_type=MESH)

    @pl.when(k > 0)
    def _():
        pl.semaphore_signal(barrier, inc=1, device_id=device(o, p - 2), device_id_type=MESH)

    target = lax.broadcasted_iota(jnp.int32, (rows, rows), 0)
    source = lax.broadcasted_iota(jnp.int32, (rows, rows), 1)
    wanted = target * arcs
    for a in range(1, arcs):
        wanted = jnp.where(target >= a * epochs, (target - a * epochs) * arcs + a, wanted)
    sort = jnp.where(source == wanted, 1.0, 0.0).astype(jnp.bfloat16)
    for lo in range(0, columns, 512):
        size = min(512, columns - lo)
        tile = jnp.dot(sort, design_ref[:, lo : lo + size], preferred_element_type=jnp.float32)
        tile = tile.astype(jnp.bfloat16)
        for a in range(arcs):
            raw_ref[a, epochs_of(o), lo : lo + size] = tile[a * epochs : (a + 1) * epochs]

    near = jnp.where(k < hops, 1, 0) + jnp.where(k > 0, 1, 0)
    pl.semaphore_wait(barrier, obs_size + near)

    sent = []

    def place(g):
        return pltpu.make_async_copy(
            raw_ref.at[:, epochs_of(o), lanes_of(core, g)], pools[g].at[p], place_sem.at[g]
        )

    def across(g):
        return pltpu.make_async_remote_copy(
            raw_ref.at[:, epochs_of(o), lanes_of(1 - core, g)], pools[g].at[p],
            across_s.at[g], across_r.at[g], device_id=device(o, other), device_id_type=MESH,
        )

    def across_in(g):
        return pltpu.make_async_remote_copy(
            pools[g].at[other], pools[g].at[other],
            across_s.at[g], across_r.at[g], device_id=device(o, other), device_id_type=MESH,
        )

    def line(g, way, s, incoming):
        if way == 0:
            pair, to = (k - 1 - s if incoming else k - s), p + 2
        else:
            pair, to = (k + 1 + s if incoming else k + s), p - 2
        window = pools[g].at[pl.ds(pair * 2, 2)]
        return pltpu.make_async_remote_copy(
            window, window, line_s.at[way, g, s], line_r.at[way, g, s],
            device_id=device(o, to), device_id_type=MESH,
        )

    def sends(way, s):
        return ((k >= s) & (k < hops)) if way == 0 else ((k + s < chips) & (k > 0))

    def receives(way, s):
        return (k - 1 - s >= 0) if way == 0 else (k + 1 + s < chips)

    def line_wait(g, s):
        for way in (0, 1):
            @pl.when(receives(way, s))
            def _():
                line(g, way, s, True).wait_recv()

    def busiest(way):
        return (k == hops - 1) if way == 0 else (k == 1)

    def relaxed(way, s):
        return sends(way, s) & jnp.logical_not(busiest(way))

    def line_send(g, s):
        for way in (0, 1):
            @pl.when(busiest(way))
            def _():
                if g >= 0:
                    before = g * hops + s - 2
                    if before >= 0:
                        line(before // hops, way, before % hops, False).wait_send()
                    line(g, way, s, False).start()

            @pl.when(relaxed(way, s))
            def _():
                own, lag = (g + 1, 2) if s == 0 else (g, 1)
                if own < chunks:
                    if own >= lag:
                        line(own - lag, way, s, False).wait_send()
                    line(own, way, s, False).start()

    def line_finish():
        for way in (0, 1):
            @pl.when(busiest(way))
            def _():
                for unit in range(max(chunks * hops - 2, 0), chunks * hops):
                    line(unit // hops, way, unit % hops, False).wait_send()

            for s in range(hops):
                @pl.when(relaxed(way, s))
                def _():
                    for g in range(max(chunks - (2 if s == 0 else 1), 0), chunks):
                        line(g, way, s, False).wait_send()

    square = obs_size == 4 and arcs == 2
    first = lax.rem(o, 2)
    beside = (o - first + 1 - first, 2 - o + 2 * first)

    def own_copy(d, owner):
        window = raw_ref.at[:, epochs_of(owner), :]
        return pltpu.make_async_remote_copy(
            window, window, own_s.at[d - 1], own_r.at[d - 1],
            device_id=device(obs_peer(d), p), device_id_type=MESH,
        )

    def own_arc(way, a, owner, slot):
        window = raw_ref.at[a, epochs_of(owner), :]
        return pltpu.make_async_remote_copy(
            window, window, own_s.at[slot], own_r.at[slot],
            device_id=device(beside[way], p), device_id_type=MESH,
        )

    def own_send(a):
        if square:
            for way in range(2):
                copy = own_arc(way, (a + way) % 2, o, 3 * way + a)
                copy.start()
                sent.append(copy)
        elif a == 0:
            for d in range(1, obs_size):
                own_copy(d, o).start()
                sent.append(own_copy(d, o))

    def own_forward():
        if square:
            for way in range(2):
                own_arc(way, way, beside[way], 3 * way).wait_recv()
            for way in range(2):
                copy = own_arc(1 - way, way, beside[way], 3 * (1 - way) + 2)
                copy.start()
                sent.append(copy)

    def own_wait():
        if square:
            for way in range(2):
                own_arc(way, 1 - way, beside[way], 3 * way + 1).wait_recv()
                own_arc(way, 1 - way, 3 - o, 3 * way + 2).wait_recv()
        else:
            for d in range(1, obs_size):
                own_copy(d, obs_source(d)).wait_recv()

    def swap(g, d, owner):
        return pltpu.make_async_remote_copy(
            stage_ref.at[g, d - 1], mixed_ref.at[g, :, epochs_of(owner), :],
            swap_s.at[g, d - 1], swap_r.at[g, d - 1],
            device_id=device(obs_peer(d), p), device_id_type=MESH,
        )

    def back(g, which):
        window = part_ref.at[g, :, :, lanes_of(which)]
        return pltpu.make_async_remote_copy(
            window, window, back_s.at[g], back_r.at[g],
            device_id=device(o, other), device_id_type=MESH,
        )

    def filter_own(begin, end):
        size = 2 * width

        @pl.loop(begin, end)
        def _(i):
            lanes = pl.ds(pl.multiple_of(i * size, size), size)
            for a in range(arcs):
                value = jnp.dot(filt_ref[a], raw_ref[a, :, lanes], preferred_element_type=jnp.float32)
                own_ref[lanes, a * arc_len : (a + 1) * arc_len] = value.T.astype(jnp.bfloat16)

    def filter_chunk(g):
        for d in range(1, obs_size):
            swap(g, d, obs_source(d)).wait_recv()
        for a in range(arcs):
            value = jnp.dot(filt_ref[a], mixed_ref[g, a], preferred_element_type=jnp.float32)
            value = value.astype(jnp.bfloat16)
            for j in range(blocks_per):
                part_ref[g, j, a * arc_len : (a + 1) * arc_len, lanes_of(core)] = (
                    value[:, j * width : (j + 1) * width]
                )
        back(g, core).start()
        sent.append(back(g, core))

    def early_product(g):
        back(g, 1 - core).wait_recv()
        for j in range(blocks_per):
            @pl.loop(0, columns // 256)
            def _(i):
                here = pl.ds(pl.multiple_of(i * 256, 256), 256)
                value = jnp.dot(own_ref[here, :], part_ref[g, j], preferred_element_type=jnp.float32)
                early_ref[j, here, g * 256 : (g + 1) * 256] = value * (1.0 / total)

    for g in range(chunks):
        place(g).start()
        across(g).start()
        sent.append(across(g))

    def ready(g):
        place(g).wait()
        across_in(g).wait_recv()

    own_send(0)
    ready(0)
    line_send(-1, 0)
    done = 0
    for g in range(chunks):
        if g + 1 < chunks:
            ready(g + 1)
        line_send(g, 0)
        if g == 0:
            build_filters(taps_ref, limit_ref, filt_ref)
        for s in range(1, hops):
            line_wait(g, s - 1)
            line_send(g, s)
            if g == 0 and s == 1:
                own_send(1)
        if g == 0 and hops < 2:
            own_send(1)
        line_wait(g, hops - 1)
        if g == min(1, chunks - 1):
            own_forward()
        for d in range(1, obs_size):
            for j in range(blocks_per):
                block = order_ref[obs_peer(d) * blocks_per + j]
                stage_ref[g, d - 1, :, :, j * width : (j + 1) * width] = pools[g][block]
            swap(g, d, o).start()
            sent.append(swap(g, d, o))
        for j in range(blocks_per):
            block = order_ref[o * blocks_per + j]
            mixed_ref[g, :, epochs_of(o), j * width : (j + 1) * width] = pools[g][block]
        if g == max(chunks - 2, 0):
            own_wait()
            filter_own(0, chunks)
            if chunks > 1:
                filter_chunk(0)
                done = 1

    made = 0
    for g in range(done, chunks):
        filter_chunk(g)
        if made < early and g < chunks - 1:
            early_product(made)
            made += 1
    for g in range(made, early):
        early_product(g)
    for g in range(early, chunks):
        back(g, 1 - core).wait_recv()
    for copy in sent:
        copy.wait_send()
    line_finish()


def product_kernel(early, own_ref, part_ref, early_ref, out_ref, late_ref, early_s, late_s):
    columns, total = own_ref.shape
    chunks, blocks_per, _, size = part_ref.shape
    split = early * size
    rest = columns - split
    bands = late_s.shape[0]
    rows = columns // bands

    def early_copy(j):
        lanes = pl.ds(j * columns, split)
        return pltpu.make_async_copy(early_ref.at[j], out_ref.at[:, lanes], early_s.at[j])

    def late_copy(i, j):
        here = pl.ds(pl.multiple_of(i * rows, rows), rows)
        lanes = pl.ds(j * columns + split, rest)
        return pltpu.make_async_copy(late_ref.at[j, here, :], out_ref.at[here, lanes], late_s.at[i, j])

    for j in range(blocks_per):
        early_copy(j).start()

    @pl.loop(0, bands)
    def _(i):
        here = pl.ds(pl.multiple_of(i * rows, rows), rows)
        for j in range(blocks_per):
            for g in range(early, chunks):
                value = jnp.dot(own_ref[here, :], part_ref[g, j], preferred_element_type=jnp.float32)
                lo = (g - early) * size
                late_ref[j, here, lo : lo + size] = value * (1.0 / total)
            late_copy(i, j).start()

    for i in range(bands):
        for j in range(blocks_per):
            late_copy(i, j).wait()
    for j in range(blocks_per):
        early_copy(j).wait()


def per_device(obs_size, par_size, design, filter_taps, band_limit, col_order):
    rows, columns = design.shape
    arcs, arc_len = filter_taps.shape
    epochs = rows // arcs
    total = arcs * arc_len
    blocks_per = par_size // obs_size
    width = LANES
    size = 2 * width
    chunks = columns // size
    hops = par_size // 2 - 1
    early = chunks // 2
    split = early * size
    bands = 3
    low, full = jnp.bfloat16, jnp.float32
    vmem, smem = pl.BlockSpec(memory_space=pltpu.VMEM), pl.BlockSpec(memory_space=pltpu.SMEM)
    anywhere = pl.BlockSpec(memory_space=pl.ANY)
    dma = pltpu.SemaphoreType.DMA
    own, part, made = pl.pallas_call(
        functools.partial(gather_kernel, obs_size, par_size, width, early),
        out_shape=(
            pltpu.VMEM((columns, total), low),
            pltpu.VMEM((chunks, blocks_per, total, size), low),
            pltpu.VMEM((blocks_per, columns, split), full),
        ),
        in_specs=[vmem, vmem, smem, smem],
        out_specs=(vmem, vmem, vmem),
        scratch_shapes=[
            pltpu.VMEM((arcs, arc_len, columns), low),
            pltpu.VMEM((arcs, arc_len, arc_len), low),
            pltpu.VMEM((chunks, obs_size - 1, arcs, epochs, blocks_per * width), low),
            pltpu.VMEM((chunks, arcs, arc_len, blocks_per * width), low),
            dma((chunks,)), dma((chunks,)), dma((chunks,)),
            dma((2, chunks, hops)), dma((2, chunks, hops)),
            dma((max(6, obs_size),)), dma((max(6, obs_size),)),
            dma((chunks, obs_size - 1)), dma((chunks, obs_size - 1)),
            dma((chunks,)), dma((chunks,)),
        ]
        + [pltpu.VMEM((par_size, arcs, epochs, width), low) for _ in range(chunks)],
        compiler_params=pltpu.CompilerParams(
            collective_id=0, has_side_effects=True, vmem_limit_bytes=36 * 1024 * 1024
        ),
    )(design, filter_taps, band_limit, col_order)
    return pl.pallas_call(
        functools.partial(product_kernel, early),
        out_shape=jax.ShapeDtypeStruct((columns, blocks_per * columns), full),
        in_specs=[vmem, vmem, vmem],
        out_specs=anywhere,
        scratch_shapes=[
            pltpu.VMEM((blocks_per, columns, columns - split), full),
            dma((blocks_per,)), dma((bands, blocks_per)),
        ],
        compiler_params=pltpu.CompilerParams(vmem_limit_bytes=24 * 1024 * 1024),
    )(own, part, made)


def solution(mesh):
    body = functools.partial(per_device, mesh.shape["obs"], mesh.shape["par"])
    placed = (P("obs", "par"), P(), P(), P())
    return jax.shard_map(body, mesh=mesh, in_specs=placed, out_specs=P("par", "obs"), check_vma=False)
```

```python
import functools

import jax
import jax.numpy as jnp
from jax import lax
from jax.experimental import pallas as pl
from jax.experimental.pallas import tpu as pltpu
from jax.sharding import PartitionSpec as P

MESH = pl.DeviceIdType.MESH
LANES = 128


def build_filters(taps_ref, limit_ref, filt_ref):
    arcs, arc_len = taps_ref.shape
    tiles = arc_len // LANES
    row = lax.broadcasted_iota(jnp.int32, (LANES, 2 * LANES), 0)
    upper = lax.broadcasted_iota(jnp.int32, (LANES, LANES), 1) >= lax.broadcasted_iota(
        jnp.int32, (LANES, LANES), 0
    )
    lag = lax.broadcasted_iota(jnp.int32, (1, arc_len), 1)
    for a in range(arcs):
        taps = taps_ref[a : a + 1, :].astype(jnp.bfloat16).astype(jnp.float32)
        taps = jnp.where(lag < limit_ref[a], taps, 0.0)
        for d in range(tiles):
            before = taps[:, (d - 1) * LANES : d * LANES] if d else jnp.zeros((1, LANES), jnp.float32)
            strip = jnp.concatenate([before, taps[:, d * LANES : (d + 1) * LANES]], axis=1)
            strip = jnp.broadcast_to(strip, (LANES, 2 * LANES))
            step = 1
            while step < LANES:
                strip = jnp.where((row & step) != 0, pltpu.roll(strip, step, 1), strip)
                step *= 2
            tile = strip[:, LANES:]
            mirrored = tile.T
            if d == 0:
                tile = jnp.where(upper, tile, mirrored)
            tile_low, mirrored_low = tile.astype(jnp.bfloat16), mirrored.astype(jnp.bfloat16)
            for i in range(tiles - d):
                lo, hi = pl.ds(i * LANES, LANES), pl.ds((i + d) * LANES, LANES)
                filt_ref[a, lo, hi] = tile_low
                if d:
                    filt_ref[a, hi, lo] = mirrored_low


def gather_kernel(
    obs_size, par_size, width, early,
    design_ref, taps_ref, limit_ref, order_ref,
    own_ref, part_ref, early_ref,
    raw_ref, filt_ref, stage_ref, mixed_ref,
    place_sem, across_s, across_r, line_s, line_r,
    own_s, own_r, swap_s, swap_r, back_s, back_r,
    *pools,
):
    arcs, arc_len, columns = raw_ref.shape
    rows = design_ref.shape[0]
    epochs = rows // arcs
    chunks = columns // (2 * width)
    total = arcs * arc_len
    blocks_per = par_size // obs_size
    chips = par_size // 2
    hops = chips - 1
    o, p = lax.axis_index("obs"), lax.axis_index("par")
    k, core = p // 2, p % 2
    other = k * 2 + 1 - core

    def obs_peer(d):
        return lax.rem(o + d, obs_size)

    def obs_source(d):
        return lax.rem(o + obs_size - d, obs_size)

    def device(obs, par):
        return {"obs": obs, "par": par}

    def epochs_of(obs):
        return pl.ds(pl.multiple_of(obs * epochs, epochs), epochs)

    def lanes_of(which, g=0):
        return pl.ds(pl.multiple_of((2 * g + which) * width, LANES), width)

    barrier = pltpu.get_barrier_semaphore()
    for d in range(1, obs_size):
        pl.semaphore_signal(barrier, inc=1, device_id=device(obs_peer(d), p), device_id_type=MESH)
    pl.semaphore_signal(barrier, inc=1, device_id=device(o, other), device_id_type=MESH)

    @pl.when(k < hops)
    def _():
        pl.semaphore_signal(barrier, inc=1, device_id=device(o, p + 2), device_id_type=MESH)

    @pl.when(k > 0)
    def _():
        pl.semaphore_signal(barrier, inc=1, device_id=device(o, p - 2), device_id_type=MESH)

    target = lax.broadcasted_iota(jnp.int32, (rows, rows), 0)
    source = lax.broadcasted_iota(jnp.int32, (rows, rows), 1)
    wanted = target * arcs
    for a in range(1, arcs):
        wanted = jnp.where(target >= a * epochs, (target - a * epochs) * arcs + a, wanted)
    sort = jnp.where(source == wanted, 1.0, 0.0).astype(jnp.bfloat16)
    for lo in range(0, columns, 512):
        size = min(512, columns - lo)
        tile = jnp.dot(sort, design_ref[:, lo : lo + size], preferred_element_type=jnp.float32)
        tile = tile.astype(jnp.bfloat16)
        for a in range(arcs):
            raw_ref[a, epochs_of(o), lo : lo + size] = tile[a * epochs : (a + 1) * epochs]

    near = jnp.where(k < hops, 1, 0) + jnp.where(k > 0, 1, 0)
    pl.semaphore_wait(barrier, obs_size + near)

    sent = []

    def place(g):
        return pltpu.make_async_copy(
            raw_ref.at[:, epochs_of(o), lanes_of(core, g)], pools[g].at[p], place_sem.at[g]
        )

    def across(g):
        return pltpu.make_async_remote_copy(
            raw_ref.at[:, epochs_of(o), lanes_of(1 - core, g)], pools[g].at[p],
            across_s.at[g], across_r.at[g], device_id=device(o, other), device_id_type=MESH,
        )

    def across_in(g):
        return pltpu.make_async_remote_copy(
            pools[g].at[other], pools[g].at[other],
            across_s.at[g], across_r.at[g], device_id=device(o, other), device_id_type=MESH,
        )

    def line(g, way, s, incoming):
        if way == 0:
            pair, to = (k - 1 - s if incoming else k - s), p + 2
        else:
            pair, to = (k + 1 + s if incoming else k + s), p - 2
        window = pools[g].at[pl.ds(pair * 2, 2)]
        return pltpu.make_async_remote_copy(
            window, window, line_s.at[way, g, s], line_r.at[way, g, s],
            device_id=device(o, to), device_id_type=MESH,
        )

    def sends(way, s):
        return ((k >= s) & (k < hops)) if way == 0 else ((k + s < chips) & (k > 0))

    def receives(way, s):
        return (k - 1 - s >= 0) if way == 0 else (k + 1 + s < chips)

    def line_wait(g, s):
        for way in (0, 1):
            @pl.when(receives(way, s))
            def _():
                line(g, way, s, True).wait_recv()

    def line_send(g, s):
        for way in (0, 1):
            @pl.when(sends(way, s))
            def _():
                line(g, way, s, False).start()

    square = obs_size == 4 and arcs == 2
    first = lax.rem(o, 2)
    beside = (o - first + 1 - first, 2 - o + 2 * first)

    def own_copy(d, owner):
        window = raw_ref.at[:, epochs_of(owner), :]
        return pltpu.make_async_remote_copy(
            window, window, own_s.at[d - 1], own_r.at[d - 1],
            device_id=device(obs_peer(d), p), device_id_type=MESH,
        )

    def own_arc(way, a, owner, slot):
        window = raw_ref.at[a, epochs_of(owner), :]
        return pltpu.make_async_remote_copy(
            window, window, own_s.at[slot], own_r.at[slot],
            device_id=device(beside[way], p), device_id_type=MESH,
        )

    def own_send():
        if square:
            for a in range(arcs):
                for way in range(2):
                    copy = own_arc(way, (a + way) % 2, o, 3 * way + a)
                    copy.start()
                    sent.append(copy)
        else:
            for d in range(1, obs_size):
                own_copy(d, o).start()
                sent.append(own_copy(d, o))

    def own_forward():
        if square:
            for way in range(2):
                own_arc(way, way, beside[way], 3 * way).wait_recv()
            for way in range(2):
                copy = own_arc(1 - way, way, beside[way], 3 * (1 - way) + 2)
                copy.start()
                sent.append(copy)

    def own_wait():
        if square:
            for way in range(2):
                own_arc(way, 1 - way, beside[way], 3 * way + 1).wait_recv()
                own_arc(way, 1 - way, 3 - o, 3 * way + 2).wait_recv()
        else:
            for d in range(1, obs_size):
                own_copy(d, obs_source(d)).wait_recv()

    def swap(g, d, owner):
        return pltpu.make_async_remote_copy(
            stage_ref.at[g, d - 1], mixed_ref.at[g, :, epochs_of(owner), :],
            swap_s.at[g, d - 1], swap_r.at[g, d - 1],
            device_id=device(obs_peer(d), p), device_id_type=MESH,
        )

    def back(g, which):
        window = part_ref.at[g, :, :, lanes_of(which)]
        return pltpu.make_async_remote_copy(
            window, window, back_s.at[g], back_r.at[g],
            device_id=device(o, other), device_id_type=MESH,
        )

    def filter_own(begin, end):
        size = 2 * width

        @pl.loop(begin, end)
        def _(i):
            lanes = pl.ds(pl.multiple_of(i * size, size), size)
            for a in range(arcs):
                value = jnp.dot(filt_ref[a], raw_ref[a, :, lanes], preferred_element_type=jnp.float32)
                own_ref[lanes, a * arc_len : (a + 1) * arc_len] = value.T.astype(jnp.bfloat16)

    def filter_chunk(g):
        for d in range(1, obs_size):
            swap(g, d, obs_source(d)).wait_recv()
        for a in range(arcs):
            value = jnp.dot(filt_ref[a], mixed_ref[g, a], preferred_element_type=jnp.float32)
            value = value.astype(jnp.bfloat16)
            for j in range(blocks_per):
                part_ref[g, j, a * arc_len : (a + 1) * arc_len, lanes_of(core)] = (
                    value[:, j * width : (j + 1) * width]
                )
        back(g, core).start()
        sent.append(back(g, core))

    def early_product(g):
        back(g, 1 - core).wait_recv()
        for j in range(blocks_per):
            @pl.loop(0, columns // 512)
            def _(i):
                here = pl.ds(pl.multiple_of(i * 512, 512), 512)
                value = jnp.dot(own_ref[here, :], part_ref[g, j], preferred_element_type=jnp.float32)
                early_ref[j, here, g * 256 : (g + 1) * 256] = value * (1.0 / total)

    for g in range(chunks):
        place(g).start()
        across(g).start()
        sent.append(across(g))

    def first_send(g):
        place(g).wait()
        across_in(g).wait_recv()
        line_send(g, 0)

    own_send()
    for g in range(min(2, chunks)):
        first_send(g)
    build_filters(taps_ref, limit_ref, filt_ref)

    done = made = 0
    for stage in range(1, chunks + hops):
        for s in range(1, hops):
            g = stage - s
            if 0 <= g < chunks:
                line_wait(g, s - 1)
                line_send(g, s)
        if stage + 1 < chunks:
            first_send(stage + 1)
        g = stage - hops
        if 0 <= g < chunks:
            line_wait(g, hops - 1)
            if g == 0:
                own_forward()
            for d in range(1, obs_size):
                for j in range(blocks_per):
                    block = order_ref[obs_peer(d) * blocks_per + j]
                    stage_ref[g, d - 1, :, :, j * width : (j + 1) * width] = pools[g][block]
                swap(g, d, o).start()
                sent.append(swap(g, d, o))
            for j in range(blocks_per):
                block = order_ref[o * blocks_per + j]
                mixed_ref[g, :, epochs_of(o), j * width : (j + 1) * width] = pools[g][block]

        left = chunks + hops - 1 - stage
        if left == 3:
            own_wait()
            filter_own(0, chunks)
        if left < 3 and done < chunks - 1 and left > 0:
            filter_chunk(done)
            done += 1
            if made < early and left == 2:
                early_product(made)
                made += 1

    for g in range(done, chunks):
        filter_chunk(g)
        if made < early - 1 and g == chunks - 3:
            early_product(made)
            made += 1
    for g in range(made, early):
        early_product(g)
    for g in range(early, chunks):
        back(g, 1 - core).wait_recv()
    for copy in sent:
        copy.wait_send()
    for g in range(chunks):
        for s in range(hops):
            for way in (0, 1):
                @pl.when(sends(way, s))
                def _():
                    line(g, way, s, False).wait_send()


def product_kernel(early, own_ref, part_ref, early_ref, out_ref, late_ref, early_s, late_s):
    columns, total = own_ref.shape
    chunks, blocks_per, _, size = part_ref.shape
    split = early * size
    rest = columns - split
    bands = late_s.shape[0]
    rows = columns // bands

    def early_copy(j):
        lanes = pl.ds(j * columns, split)
        return pltpu.make_async_copy(early_ref.at[j], out_ref.at[:, lanes], early_s.at[j])

    def late_copy(i, j):
        here = pl.ds(pl.multiple_of(i * rows, rows), rows)
        lanes = pl.ds(j * columns + split, rest)
        return pltpu.make_async_copy(late_ref.at[j, here, :], out_ref.at[here, lanes], late_s.at[i, j])

    for j in range(blocks_per):
        early_copy(j).start()

    @pl.loop(0, bands)
    def _(i):
        here = pl.ds(pl.multiple_of(i * rows, rows), rows)
        for j in range(blocks_per):
            for g in range(early, chunks):
                value = jnp.dot(own_ref[here, :], part_ref[g, j], preferred_element_type=jnp.float32)
                lo = (g - early) * size
                late_ref[j, here, lo : lo + size] = value * (1.0 / total)
            late_copy(i, j).start()

    for i in range(bands):
        for j in range(blocks_per):
            late_copy(i, j).wait()
    for j in range(blocks_per):
        early_copy(j).wait()


def per_device(obs_size, par_size, design, filter_taps, band_limit, col_order):
    rows, columns = design.shape
    arcs, arc_len = filter_taps.shape
    epochs = rows // arcs
    total = arcs * arc_len
    blocks_per = par_size // obs_size
    width = LANES
    size = 2 * width
    chunks = columns // size
    hops = par_size // 2 - 1
    early = chunks // 2
    split = early * size
    bands = 3
    low, full = jnp.bfloat16, jnp.float32
    vmem, smem = pl.BlockSpec(memory_space=pltpu.VMEM), pl.BlockSpec(memory_space=pltpu.SMEM)
    anywhere = pl.BlockSpec(memory_space=pl.ANY)
    dma = pltpu.SemaphoreType.DMA
    own, part, made = pl.pallas_call(
        functools.partial(gather_kernel, obs_size, par_size, width, early),
        out_shape=(
            pltpu.VMEM((columns, total), low),
            pltpu.VMEM((chunks, blocks_per, total, size), low),
            pltpu.VMEM((blocks_per, columns, split), full),
        ),
        in_specs=[vmem, vmem, smem, smem],
        out_specs=(vmem, vmem, vmem),
        scratch_shapes=[
            pltpu.VMEM((arcs, arc_len, columns), low),
            pltpu.VMEM((arcs, arc_len, arc_len), low),
            pltpu.VMEM((chunks, obs_size - 1, arcs, epochs, blocks_per * width), low),
            pltpu.VMEM((chunks, arcs, arc_len, blocks_per * width), low),
            dma((chunks,)), dma((chunks,)), dma((chunks,)),
            dma((2, chunks, hops)), dma((2, chunks, hops)),
            dma((max(6, obs_size),)), dma((max(6, obs_size),)),
            dma((chunks, obs_size - 1)), dma((chunks, obs_size - 1)),
            dma((chunks,)), dma((chunks,)),
        ]
        + [pltpu.VMEM((par_size, arcs, epochs, width), low) for _ in range(chunks)],
        compiler_params=pltpu.CompilerParams(
            collective_id=0, has_side_effects=True, vmem_limit_bytes=36 * 1024 * 1024
        ),
    )(design, filter_taps, band_limit, col_order)
    return pl.pallas_call(
        functools.partial(product_kernel, early),
        out_shape=jax.ShapeDtypeStruct((columns, blocks_per * columns), full),
        in_specs=[vmem, vmem, vmem],
        out_specs=anywhere,
        scratch_shapes=[
            pltpu.VMEM((blocks_per, columns, columns - split), full),
            dma((blocks_per,)), dma((bands, blocks_per)),
        ],
        compiler_params=pltpu.CompilerParams(vmem_limit_bytes=24 * 1024 * 1024),
    )(own, part, made)


def solution(mesh):
    body = functools.partial(per_device, mesh.shape["obs"], mesh.shape["par"])
    placed = (P("obs", "par"), P(), P(), P())
    return jax.shard_map(body, mesh=mesh, in_specs=placed, out_specs=P("par", "obs"), check_vma=False)
```

```python
import functools

import jax
import jax.numpy as jnp
from jax import lax
from jax.experimental import pallas as pl
from jax.experimental.pallas import tpu as pltpu
from jax.sharding import PartitionSpec as P

MESH = pl.DeviceIdType.MESH
LANES = 128


def build_filters(taps_ref, limit_ref, filt_ref):
    arcs, arc_len = taps_ref.shape
    tiles = arc_len // LANES
    row = lax.broadcasted_iota(jnp.int32, (LANES, 2 * LANES), 0)
    upper = lax.broadcasted_iota(jnp.int32, (LANES, LANES), 1) >= lax.broadcasted_iota(
        jnp.int32, (LANES, LANES), 0
    )
    lag = lax.broadcasted_iota(jnp.int32, (1, arc_len), 1)
    for a in range(arcs):
        taps = taps_ref[a : a + 1, :].astype(jnp.bfloat16).astype(jnp.float32)
        taps = jnp.where(lag < limit_ref[a], taps, 0.0)
        for d in range(tiles):
            before = taps[:, (d - 1) * LANES : d * LANES] if d else jnp.zeros((1, LANES), jnp.float32)
            strip = jnp.concatenate([before, taps[:, d * LANES : (d + 1) * LANES]], axis=1)
            strip = jnp.broadcast_to(strip, (LANES, 2 * LANES))
            step = 1
            while step < LANES:
                strip = jnp.where((row & step) != 0, pltpu.roll(strip, step, 1), strip)
                step *= 2
            tile = strip[:, LANES:]
            mirrored = tile.T
            if d == 0:
                tile = jnp.where(upper, tile, mirrored)
            tile_low, mirrored_low = tile.astype(jnp.bfloat16), mirrored.astype(jnp.bfloat16)
            for i in range(tiles - d):
                lo, hi = pl.ds(i * LANES, LANES), pl.ds((i + d) * LANES, LANES)
                filt_ref[a, lo, hi] = tile_low
                if d:
                    filt_ref[a, hi, lo] = mirrored_low


def gather_kernel(
    obs_size, par_size, width, early,
    design_ref, taps_ref, limit_ref, order_ref,
    own_ref, part_ref, early_ref,
    raw_ref, filt_ref, stage_ref, mixed_ref,
    place_sem, across_s, across_r, line_s, line_r,
    own_s, own_r, swap_s, swap_r, back_s, back_r,
    *pools,
):
    arcs, arc_len, columns = raw_ref.shape
    rows = design_ref.shape[0]
    epochs = rows // arcs
    chunks = columns // (2 * width)
    total = arcs * arc_len
    blocks_per = par_size // obs_size
    chips = par_size // 2
    hops = chips - 1
    o, p = lax.axis_index("obs"), lax.axis_index("par")
    k, core = p // 2, p % 2
    other = k * 2 + 1 - core

    def obs_peer(d):
        return lax.rem(o + d, obs_size)

    def obs_source(d):
        return lax.rem(o + obs_size - d, obs_size)

    def device(obs, par):
        return {"obs": obs, "par": par}

    def epochs_of(obs):
        return pl.ds(pl.multiple_of(obs * epochs, epochs), epochs)

    def lanes_of(which, g=0):
        return pl.ds(pl.multiple_of((2 * g + which) * width, LANES), width)

    barrier = pltpu.get_barrier_semaphore()
    for d in range(1, obs_size):
        pl.semaphore_signal(barrier, inc=1, device_id=device(obs_peer(d), p), device_id_type=MESH)
    pl.semaphore_signal(barrier, inc=1, device_id=device(o, other), device_id_type=MESH)

    @pl.when(k < hops)
    def _():
        pl.semaphore_signal(barrier, inc=1, device_id=device(o, p + 2), device_id_type=MESH)

    @pl.when(k > 0)
    def _():
        pl.semaphore_signal(barrier, inc=1, device_id=device(o, p - 2), device_id_type=MESH)

    target = lax.broadcasted_iota(jnp.int32, (rows, rows), 0)
    source = lax.broadcasted_iota(jnp.int32, (rows, rows), 1)
    wanted = target * arcs
    for a in range(1, arcs):
        wanted = jnp.where(target >= a * epochs, (target - a * epochs) * arcs + a, wanted)
    sort = jnp.where(source == wanted, 1.0, 0.0).astype(jnp.bfloat16)
    for lo in range(0, columns, 512):
        size = min(512, columns - lo)
        tile = jnp.dot(sort, design_ref[:, lo : lo + size], preferred_element_type=jnp.float32)
        tile = tile.astype(jnp.bfloat16)
        for a in range(arcs):
            raw_ref[a, epochs_of(o), lo : lo + size] = tile[a * epochs : (a + 1) * epochs]

    near = jnp.where(k < hops, 1, 0) + jnp.where(k > 0, 1, 0)
    pl.semaphore_wait(barrier, obs_size + near)

    sent = []

    def place(g):
        return pltpu.make_async_copy(
            raw_ref.at[:, epochs_of(o), lanes_of(core, g)], pools[g].at[p], place_sem.at[g]
        )

    def across(g):
        return pltpu.make_async_remote_copy(
            raw_ref.at[:, epochs_of(o), lanes_of(1 - core, g)], pools[g].at[p],
            across_s.at[g], across_r.at[g], device_id=device(o, other), device_id_type=MESH,
        )

    def across_in(g):
        return pltpu.make_async_remote_copy(
            pools[g].at[other], pools[g].at[other],
            across_s.at[g], across_r.at[g], device_id=device(o, other), device_id_type=MESH,
        )

    def line(g, way, s, incoming):
        if way == 0:
            pair, to = (k - 1 - s if incoming else k - s), p + 2
        else:
            pair, to = (k + 1 + s if incoming else k + s), p - 2
        window = pools[g].at[pl.ds(pair * 2, 2)]
        return pltpu.make_async_remote_copy(
            window, window, line_s.at[way, g, s], line_r.at[way, g, s],
            device_id=device(o, to), device_id_type=MESH,
        )

    def sends(way, s):
        return ((k >= s) & (k < hops)) if way == 0 else ((k + s < chips) & (k > 0))

    def receives(way, s):
        return (k - 1 - s >= 0) if way == 0 else (k + 1 + s < chips)

    def line_wait(g, s):
        for way in (0, 1):
            @pl.when(receives(way, s))
            def _():
                line(g, way, s, True).wait_recv()

    def line_send(g, s):
        for way in (0, 1):
            @pl.when(sends(way, s))
            def _():
                line(g, way, s, False).start()

    square = obs_size == 4 and arcs == 2
    first = lax.rem(o, 2)
    beside = (o - first + 1 - first, 2 - o + 2 * first)

    def own_copy(d, owner):
        window = raw_ref.at[:, epochs_of(owner), :]
        return pltpu.make_async_remote_copy(
            window, window, own_s.at[d - 1], own_r.at[d - 1],
            device_id=device(obs_peer(d), p), device_id_type=MESH,
        )

    def own_arc(way, a, owner, slot):
        window = raw_ref.at[a, epochs_of(owner), :]
        return pltpu.make_async_remote_copy(
            window, window, own_s.at[slot], own_r.at[slot],
            device_id=device(beside[way], p), device_id_type=MESH,
        )

    def own_send():
        if square:
            for a in range(arcs):
                for way in range(2):
                    copy = own_arc(way, (a + way) % 2, o, 3 * way + a)
                    copy.start()
                    sent.append(copy)
        else:
            for d in range(1, obs_size):
                own_copy(d, o).start()
                sent.append(own_copy(d, o))

    def own_forward():
        if square:
            for way in range(2):
                own_arc(way, way, beside[way], 3 * way).wait_recv()
            for way in range(2):
                copy = own_arc(1 - way, way, beside[way], 3 * (1 - way) + 2)
                copy.start()
                sent.append(copy)

    def own_wait():
        if square:
            for way in range(2):
                own_arc(way, 1 - way, beside[way], 3 * way + 1).wait_recv()
                own_arc(way, 1 - way, 3 - o, 3 * way + 2).wait_recv()
        else:
            for d in range(1, obs_size):
                own_copy(d, obs_source(d)).wait_recv()

    def swap(g, d, owner):
        return pltpu.make_async_remote_copy(
            stage_ref.at[g, d - 1], mixed_ref.at[g, :, epochs_of(owner), :],
            swap_s.at[g, d - 1], swap_r.at[g, d - 1],
            device_id=device(obs_peer(d), p), device_id_type=MESH,
        )

    def back(g, which):
        window = part_ref.at[g, :, :, lanes_of(which)]
        return pltpu.make_async_remote_copy(
            window, window, back_s.at[g], back_r.at[g],
            device_id=device(o, other), device_id_type=MESH,
        )

    def filter_own(begin, end):
        size = 2 * width

        @pl.loop(begin, end)
        def _(i):
            lanes = pl.ds(pl.multiple_of(i * size, size), size)
            for a in range(arcs):
                value = jnp.dot(filt_ref[a], raw_ref[a, :, lanes], preferred_element_type=jnp.float32)
                own_ref[lanes, a * arc_len : (a + 1) * arc_len] = value.T.astype(jnp.bfloat16)

    def filter_chunk(g):
        for d in range(1, obs_size):
            swap(g, d, obs_source(d)).wait_recv()
        for a in range(arcs):
            value = jnp.dot(filt_ref[a], mixed_ref[g, a], preferred_element_type=jnp.float32)
            value = value.astype(jnp.bfloat16)
            for j in range(blocks_per):
                part_ref[g, j, a * arc_len : (a + 1) * arc_len, lanes_of(core)] = (
                    value[:, j * width : (j + 1) * width]
                )
        back(g, core).start()
        sent.append(back(g, core))

    def early_product(g):
        back(g, 1 - core).wait_recv()
        for j in range(blocks_per):
            @pl.loop(0, columns // 512)
            def _(i):
                here = pl.ds(pl.multiple_of(i * 512, 512), 512)
                value = jnp.dot(own_ref[here, :], part_ref[g, j], preferred_element_type=jnp.float32)
                early_ref[j, here, g * 256 : (g + 1) * 256] = value * (1.0 / total)

    for g in range(chunks):
        place(g).start()
        across(g).start()
        sent.append(across(g))

    def first_send(g):
        place(g).wait()
        across_in(g).wait_recv()
        line_send(g, 0)

    own_send()
    for g in range(min(2, chunks)):
        first_send(g)
    build_filters(taps_ref, limit_ref, filt_ref)

    done = made = 0
    for stage in range(1, chunks + hops):
        for s in range(1, hops):
            g = stage - s
            if 0 <= g < chunks:
                line_wait(g, s - 1)
                line_send(g, s)
        if stage + 1 < chunks:
            first_send(stage + 1)
        g = stage - hops
        if 0 <= g < chunks:
            line_wait(g, hops - 1)
            if g == 0:
                own_forward()
            for d in range(1, obs_size):
                for j in range(blocks_per):
                    block = order_ref[obs_peer(d) * blocks_per + j]
                    stage_ref[g, d - 1, :, :, j * width : (j + 1) * width] = pools[g][block]
                swap(g, d, o).start()
                sent.append(swap(g, d, o))
            for j in range(blocks_per):
                block = order_ref[o * blocks_per + j]
                mixed_ref[g, :, epochs_of(o), j * width : (j + 1) * width] = pools[g][block]

        left = chunks + hops - 1 - stage
        if left == 3:
            own_wait()
            filter_own(0, chunks)
        if left == 2 and done < chunks - 1:
            filter_chunk(done)
            done += 1
            if made < early:
                early_product(made)
                made += 1
        if left == 1:
            while done < min(3, chunks - 2):
                filter_chunk(done)
                done += 1

    for g in range(done, chunks):
        filter_chunk(g)
        if made < early - 1 and g == chunks - 3:
            early_product(made)
            made += 1
    for g in range(made, early):
        early_product(g)
    for g in range(early, chunks):
        back(g, 1 - core).wait_recv()
    for copy in sent:
        copy.wait_send()
    for g in range(chunks):
        for s in range(hops):
            for way in (0, 1):
                @pl.when(sends(way, s))
                def _():
                    line(g, way, s, False).wait_send()


def product_kernel(early, own_ref, part_ref, early_ref, out_ref, late_ref, early_s, late_s):
    columns, total = own_ref.shape
    chunks, blocks_per, _, size = part_ref.shape
    split = early * size
    rest = columns - split
    bands = late_s.shape[0]
    rows = columns // bands

    def early_copy(j):
        lanes = pl.ds(j * columns, split)
        return pltpu.make_async_copy(early_ref.at[j], out_ref.at[:, lanes], early_s.at[j])

    def late_copy(i, j):
        here = pl.ds(pl.multiple_of(i * rows, rows), rows)
        lanes = pl.ds(j * columns + split, rest)
        return pltpu.make_async_copy(late_ref.at[j, here, :], out_ref.at[here, lanes], late_s.at[i, j])

    for j in range(blocks_per):
        early_copy(j).start()

    @pl.loop(0, bands)
    def _(i):
        here = pl.ds(pl.multiple_of(i * rows, rows), rows)
        for j in range(blocks_per):
            for g in range(early, chunks):
                value = jnp.dot(own_ref[here, :], part_ref[g, j], preferred_element_type=jnp.float32)
                lo = (g - early) * size
                late_ref[j, here, lo : lo + size] = value * (1.0 / total)
            late_copy(i, j).start()

    for i in range(bands):
        for j in range(blocks_per):
            late_copy(i, j).wait()
    for j in range(blocks_per):
        early_copy(j).wait()


def per_device(obs_size, par_size, design, filter_taps, band_limit, col_order):
    rows, columns = design.shape
    arcs, arc_len = filter_taps.shape
    epochs = rows // arcs
    total = arcs * arc_len
    blocks_per = par_size // obs_size
    width = LANES
    size = 2 * width
    chunks = columns // size
    hops = par_size // 2 - 1
    early = chunks // 2
    split = early * size
    bands = 3
    low, full = jnp.bfloat16, jnp.float32
    vmem, smem = pl.BlockSpec(memory_space=pltpu.VMEM), pl.BlockSpec(memory_space=pltpu.SMEM)
    anywhere = pl.BlockSpec(memory_space=pl.ANY)
    dma = pltpu.SemaphoreType.DMA
    own, part, made = pl.pallas_call(
        functools.partial(gather_kernel, obs_size, par_size, width, early),
        out_shape=(
            pltpu.VMEM((columns, total), low),
            pltpu.VMEM((chunks, blocks_per, total, size), low),
            pltpu.VMEM((blocks_per, columns, split), full),
        ),
        in_specs=[vmem, vmem, smem, smem],
        out_specs=(vmem, vmem, vmem),
        scratch_shapes=[
            pltpu.VMEM((arcs, arc_len, columns), low),
            pltpu.VMEM((arcs, arc_len, arc_len), low),
            pltpu.VMEM((chunks, obs_size - 1, arcs, epochs, blocks_per * width), low),
            pltpu.VMEM((chunks, arcs, arc_len, blocks_per * width), low),
            dma((chunks,)), dma((chunks,)), dma((chunks,)),
            dma((2, chunks, hops)), dma((2, chunks, hops)),
            dma((max(6, obs_size),)), dma((max(6, obs_size),)),
            dma((chunks, obs_size - 1)), dma((chunks, obs_size - 1)),
            dma((chunks,)), dma((chunks,)),
        ]
        + [pltpu.VMEM((par_size, arcs, epochs, width), low) for _ in range(chunks)],
        compiler_params=pltpu.CompilerParams(
            collective_id=0, has_side_effects=True, vmem_limit_bytes=36 * 1024 * 1024
        ),
    )(design, filter_taps, band_limit, col_order)
    return pl.pallas_call(
        functools.partial(product_kernel, early),
        out_shape=jax.ShapeDtypeStruct((columns, blocks_per * columns), full),
        in_specs=[vmem, vmem, vmem],
        out_specs=anywhere,
        scratch_shapes=[
            pltpu.VMEM((blocks_per, columns, columns - split), full),
            dma((blocks_per,)), dma((bands, blocks_per)),
        ],
        compiler_params=pltpu.CompilerParams(vmem_limit_bytes=24 * 1024 * 1024),
    )(own, part, made)


def solution(mesh):
    body = functools.partial(per_device, mesh.shape["obs"], mesh.shape["par"])
    placed = (P("obs", "par"), P(), P(), P())
    return jax.shard_map(body, mesh=mesh, in_specs=placed, out_specs=P("par", "obs"), check_vma=False)
```
